128 devices in a mesh: dp: 16 (over x, y), seq: 8 (over z, core).
Axes of the slice: x: 4, y: 4, z: 4, core: 2. Of those that a mesh axis runs over, the one named last changes fastest.
Arguments:
- tokens: bfloat16 [16384, 4096], P(('dp', 'seq')), may hold values from -6 to 6
- norm_gain: float32 [4096], replicated, may hold values from 0.1 to 1.9
- send_order: int32 [128, 128], P(('dp', 'seq')), may hold values from 0 to 127, each once within a row
- segment_ids: int32 [16, 1024], P('dp'), may hold values from 0 to 7, never falling along the last dimension, each value on 1 to 512 neighbouring positions
- w_query: bfloat16 [4096, 4096], P('dp', 'seq'), as said below
- w_key: bfloat16 [4096, 512], P('dp'), as said below
- w_value: bfloat16 [4096, 512], P('dp'), may hold values from -0.09375 to 0.09375
- w_out: bfloat16 [4096, 4096], P('seq', 'dp'), may hold values from -0.09375 to 0.09375
Outputs:
- attended: bfloat16 [16384, 4096], P(('dp', 'seq'))
The draws below stay inside these ranges and needn't reach their ends.
Inputs may be any that keep to these rules, and one draw needn't show every extreme that they name: `send_order`: each row names every local row once. `segment_ids`: ids never fall along a row; each document holds 1 to 512 tokens and one holds exactly that many. `w_query`: entries lie within -12 and 12 divided by the square root of 4096. `w_key`: entries lie within -12 and 12 divided by the square root of 4096.
All inputs are finite; a program needn't handle non-finite values.
Results may differ from the reference program's by a relative error of at most 0.0085.
The reference program's roundings to bfloat16 on the way (of `normed`, `packed`, `probs`, `heads_out` and `projected`) count: a program that leaves them out, or rounds other values in their place, can miss the bound.
Values may be sent and summed in bfloat16 or wider, within the bound.
A program may use at most 128 MiB of HBM per device.

```python
import math
import jax
import jax.numpy as jnp
import numpy as np
from jax import lax

D = 4096
H = 32
G = 4
HD = 128
TOK_DEV = 128
GT = 1024
TOKENS = 16384
N_DP = 16
N_SEQ = 8


def draw_w_query(key, part):
    key = jax.random.fold_in(key, 11)
    values = jax.random.truncated_normal(key, -4.0, 4.0, (D, H * HD), jnp.float32) / math.sqrt(D)
    return values.astype(jnp.bfloat16)


def draw_w_key(key, part):
    key = jax.random.fold_in(key, 23)
    values = jax.random.truncated_normal(key, -4.0, 4.0, (D, G * HD), jnp.float32) / math.sqrt(D)
    return values.astype(jnp.bfloat16)


def block_scale(own_key, shape, shards, low, high):
    def one(axis_at, parts):
        heights = jax.random.uniform(jax.random.fold_in(jax.random.fold_in(own_key, 6), axis_at), (parts,), jnp.float32, low / len(shards), high / len(shards))
        return jnp.repeat(jnp.exp(heights), shape[axis_at] // parts).reshape((-1,) + (1,) * (len(shape) - axis_at - 1))

    level = one(*shards[0])
    for cut in shards[1:]:
        level = level * one(*cut)
    return level


def length_profile(amount, total, most, skew):
    loads = [(1 << 20) // math.isqrt(rank ** skew) + 1 for rank in range(2, amount + 1)]
    rest, given = total - most - (amount - 1), [1] * (amount - 1)
    while rest > 0:
        movable = [i for i in range(amount - 1) if given[i] < most]
        whole, budget = sum([loads[i] for i in movable]), rest
        for i in movable:
            addition = min(most - given[i], max(1, budget * loads[i] // whole), rest)
            given[i] = given[i] + addition
            rest = rest - addition
    return np.array([most] + given)


def ragged_sizes(key, count, total, bound, lean):
    if count == 2:
        one = jax.random.randint(key, (), max(1, total - bound), min(bound, total - 1) + 1)
        return jnp.stack([one, total - one])
    tallies = jnp.asarray(length_profile(count, total, bound, lean), jnp.int32)
    twos = (count - 1) // 2
    giver, receiver = tallies[1:1 + 2 * twos:2], tallies[2:2 + 2 * twos:2]
    slack = jnp.minimum(giver - 1, bound - receiver)
    passed = jax.random.randint(jax.random.fold_in(key, 1), (twos,), 0, 1 << 20) % (slack + 1)
    tallies = tallies.at[1:1 + 2 * twos:2].set(giver - passed).at[2:2 + 2 * twos:2].set(receiver + passed)
    return tallies[jax.random.permutation(jax.random.fold_in(key, 2), count)]


def scatter_about(stream_key, extent, deviation, bound, split=(), kind=jnp.bfloat16):
    factor_of = block_scale(stream_key, extent, split, -0.22, 0.18) if split else 1.0
    values = jax.random.normal(stream_key, extent, jnp.float32) * deviation * factor_of
    return jnp.minimum(jnp.maximum(values, -bound), bound).astype(kind)


def setup_inputs(seed: int = 0) -> dict:
    arg_keys = jax.random.split(jax.random.key(seed), 9)
    tokens = scatter_about(arg_keys[0], (TOKENS, D), 1.0, 6.0, ((0, 128),))
    norm_gain = jnp.clip(1.0 + 0.18 * jax.random.normal(arg_keys[1], (D,), jnp.float32), 0.1, 1.9)
    send_order = jax.vmap(lambda own: jax.random.permutation(own, TOK_DEV))(jax.random.split(arg_keys[2], (N_DP * N_SEQ))).reshape((N_DP * N_SEQ, TOK_DEV)).astype(jnp.int32)
    segment_ids = jax.vmap(lambda own: jnp.searchsorted(jnp.cumsum(ragged_sizes(own, 8, GT, TOK_DEV * N_SEQ // 2, 2)), jnp.arange(GT), side="right"))(jax.random.split(arg_keys[3], N_DP)).reshape((N_DP, GT)).astype(jnp.int32)
    w_query = draw_w_query(jax.random.fold_in(arg_keys[8], 71), 0)
    w_key = draw_w_key(jax.random.fold_in(arg_keys[8], 71), 0)
    w_value = scatter_about(arg_keys[6], (D, G * HD), D ** -0.5, 0.09375, ((0, 16),))
    w_out = scatter_about(arg_keys[7], (H * HD, D), (H * HD) ** -0.5, 0.09375, ((0, 8), (1, 16)))
    return {"tokens": tokens, "norm_gain": norm_gain, "send_order": send_order, "segment_ids": segment_ids, "w_query": w_query, "w_key": w_key, "w_value": w_value, "w_out": w_out}


def reference(tokens, norm_gain, send_order, segment_ids, w_query, w_key, w_value, w_out):
    wide = tokens.astype(jnp.float32)
    square = lax.optimization_barrier(jnp.mean(wide * wide, axis=1, keepdims=True))
    normed = (wide * lax.rsqrt(square + 1e-05) * norm_gain[None, :]).astype(jnp.bfloat16)
    piece = TOK_DEV // N_DP
    dev_rows = normed.reshape(N_DP * N_SEQ, TOK_DEV, D)
    permuted = jnp.take_along_axis(dev_rows, send_order.astype(jnp.int32)[:, :, None], axis=1)
    packed = permuted.reshape(N_DP, N_SEQ, N_DP, piece, D).transpose(2, 1, 0, 3, 4).reshape(N_DP, GT, D)
    scale = HD ** (-0.5)
    per_kv = H // G

    def one_group(inputs):
        rows_g, seg = inputs
        query = jnp.dot(rows_g, w_query, preferred_element_type=jnp.float32).astype(jnp.bfloat16)
        key = jnp.dot(rows_g, w_key, preferred_element_type=jnp.float32).astype(jnp.bfloat16)
        value = jnp.dot(rows_g, w_value, preferred_element_type=jnp.float32).astype(jnp.bfloat16)
        places = jnp.arange(GT, dtype=jnp.int32)
        visible = (seg[:, None] == seg[None, :]) & (places[:, None] >= places[None, :])

        def one_head(head):
            kv_head = head // per_kv
            q_part = lax.dynamic_slice_in_dim(query, head * HD, HD, 1)
            k_part = lax.dynamic_slice_in_dim(key, kv_head * HD, HD, 1)
            v_part = lax.dynamic_slice_in_dim(value, kv_head * HD, HD, 1)
            scores = jnp.dot(q_part, k_part.T, preferred_element_type=jnp.float32) * scale
            scores = jnp.where(visible, scores, -jnp.inf)
            top = lax.optimization_barrier(jnp.max(scores, axis=1, keepdims=True))
            weights = jnp.exp(scores - top)
            probs = (weights / lax.optimization_barrier(jnp.sum(weights, axis=1, keepdims=True))).astype(jnp.bfloat16)
            return jnp.dot(probs, v_part, preferred_element_type=jnp.float32).astype(jnp.bfloat16)
        heads = lax.map(one_head, jnp.arange(H, dtype=jnp.int32))
        heads_out = heads.transpose(1, 0, 2).reshape(GT, H * HD)
        return jnp.dot(heads_out, w_out, preferred_element_type=jnp.float32).astype(jnp.bfloat16)
    projected = lax.map(one_group, (packed, segment_ids))
    back = projected.reshape(N_DP, N_SEQ, N_DP, piece, D).transpose(2, 1, 0, 3, 4).reshape(N_DP * N_SEQ, TOK_DEV, D)

    def restore(rows_d, order_d):
        return jnp.zeros_like(rows_d).at[order_d].set(rows_d)
    home = jax.vmap(restore)(back, send_order.astype(jnp.int32))
    return home.reshape(TOKENS, D)
```

```python
import jax
import jax.numpy as jnp
from jax import lax
from jax.experimental import pallas as pl
from jax.experimental.pallas import tpu as pltpu
from jax.sharding import PartitionSpec as P

BF = jnp.bfloat16
F32 = jnp.float32
MESH = pl.DeviceIdType.MESH
NEG = float("-inf")
EXP_SCALE = 128 ** (-0.5) * 1.4426950408889634

M_SIB_ROWS = 0
M_SIB_WO = 1
M_SIB_KV = 2
M_SIB_X = 3
M_SIB_HO = 7
M_A2A = 11
M_Z = 27
M_W = 39
M_WO = 71
M_OPP = 103
M_FIN = 107
M_HOME = 115
M_COUNT = 147


class Gather:
    def __init__(self, base, view, rows, at, message):
        self.base, self.view, self.rows, self.at, self.message = base, view, rows, at, message

    def part(self, h, d1, d2, quarter=None):
        half = self.rows // 2
        if quarter is None:
            return self.view(self.at(h, d1, d2), h * half, half)
        return self.view(self.at(h, d1, d2), h * half + quarter * (half // 2), half // 2)

    def send(self, h, m, ref, d1, d2):
        self.message(self.base + 16 * h + m, ref, ref, (self.at(h, d1, d2), None)).start()

    def recv(self, h, m, ref):
        self.message(self.base + 16 * h + m, ref, ref, None).wait_recv()

    def own(self):
        for h in range(2):
            mine = self.part(h, 0, 0)
            self.send(h, 0, mine, 1, 0)
            self.send(h, 1, mine, -1, 0)
            self.send(h, 4, mine, 0, 1)
            self.send(h, 8, mine, 0, -1)

    def first(self):
        for h in range(2):
            ref = self.part(h, -1, 0)
            self.recv(h, 0, ref)
            self.send(h, 2, self.part(h, -1, 0, 0), 1, 0)
            self.send(h, 5, ref, 0, 1)
            self.send(h, 9, ref, 0, -1)
        for h in range(2):
            ref = self.part(h, 1, 0)
            self.recv(h, 1, ref)
            self.send(h, 3, self.part(h, 1, 0, 1), -1, 0)
            self.send(h, 6, ref, 0, 1)
            self.send(h, 10, ref, 0, -1)
        for h in range(2):
            ref = self.part(h, 0, -1)
            self.recv(h, 4, ref)
            self.send(h, 12, ref, 0, 1)
            self.recv(h, 8, self.part(h, 0, 1))

    def second(self):
        for h in range(2):
            self.recv(h, 2, self.part(h, 2, 0, 0))
            self.recv(h, 3, self.part(h, 2, 0, 1))
            ref = self.part(h, 2, 0)
            self.send(h, 7, ref, 0, 1)
            self.send(h, 11, ref, 0, -1)

    def third(self):
        for h in range(2):
            ref = self.part(h, -1, -1)
            self.recv(h, 5, ref)
            self.send(h, 13, ref, 0, 1)
            ref = self.part(h, 1, 1)
            self.recv(h, 10, ref)
            self.send(h, 14, ref, 0, -1)
        for h in range(2):
            self.recv(h, 9, self.part(h, -1, 1))
            self.recv(h, 6, self.part(h, 1, -1))
            ref = self.part(h, 2, 1)
            self.recv(h, 11, ref)
            self.send(h, 15, ref, 0, -1)
            self.recv(h, 7, self.part(h, 2, -1))

    def last(self):
        for h in range(2):
            self.recv(h, 12, self.part(h, 0, 2))
            self.recv(h, 13, self.part(h, -1, 2))
            self.recv(h, 14, self.part(h, 1, 2))
            self.recv(h, 15, self.part(h, 2, 2))

    def drain(self):
        for h in range(2):
            for m in range(16):
                ref = self.part(h, 0, 0, 0 if m in (2, 3) else None)
                self.message(self.base + 16 * h + m, ref, ref, None).wait_send()


def kernel(
    tok, gain, order, seg, wq, wk, wv, wo, out,
    x_buf, nb, sib, s_buf, wall, wob, qkv, ho, bias, p32, snd, opr, fin, fs, r_buf, pick,
    lsem, ssem, rsem,
):
    dp = lax.axis_index("dp")
    sq = lax.axis_index("seq")
    x, y = lax.div(dp, 4), lax.rem(dp, 4)
    z, c = lax.div(sq, 2), lax.rem(sq, 2)
    other = 1 - c

    def ring(v):
        return {0: v, 1: lax.rem(v + 1, 4), 2: lax.rem(v + 2, 4), -1: lax.rem(v + 3, 4), 3: lax.rem(v + 3, 4)}

    xr, yr, zr = ring(x), ring(y), ring(z)

    def plane(kx, ky):
        return xr[kx] * 4 + yr[ky]

    def message(index, src, dst, dev):
        if dev is None:
            dev = (dp, z * 2 + other)
        elif dev[1] is None:
            dev = (dev[0], sq)
        return pltpu.make_async_remote_copy(
            src_ref=src, dst_ref=dst, send_sem=ssem.at[index], recv_sem=rsem.at[index],
            device_id=dev, device_id_type=MESH,
        )

    sibling = (dp, z * 2 + other)
    z_up, z_down = (dp, zr[1] * 2 + c), (dp, zr[-1] * 2 + c)

    barrier = pltpu.get_barrier_semaphore()
    greeted = [sibling, z_up, z_down]
    for kx in range(4):
        for ky in range(4):
            if kx or ky:
                greeted.append((plane(kx, ky), sq))
                greeted.append((plane(kx, ky), z * 2 + other))
    for dev in greeted:
        pl.semaphore_signal(barrier, inc=1, device_id=dev, device_id_type=MESH)

    load_q = pltpu.make_async_copy(wq, wall.at[dp, :, pl.ds(128, 512)], lsem.at[0])
    load_q.start()
    load_o = pltpu.make_async_copy(
        wo.at[:, pl.ds(pl.multiple_of(c * 128, 128), 128)],
        wob.at[dp, pl.ds(pl.multiple_of(c * 512, 512), 512), :], lsem.at[2])
    load_o.start()
    kv_cols = pl.ds(pl.multiple_of(z * 128, 128), 128)

    @pl.when(c == 0)
    def _():
        load = pltpu.make_async_copy(wk.at[:, kv_cols], wall.at[dp, :, pl.ds(0, 128)], lsem.at[1])
        load.start()
        load.wait()

    @pl.when(c == 1)
    def _():
        load = pltpu.make_async_copy(wv.at[:, kv_cols], wall.at[dp, :, pl.ds(640, 128)], lsem.at[1])
        load.start()
        load.wait()

    load_q.wait()
    pl.semaphore_wait(barrier, len(greeted))

    def at(h, d1, d2):
        return xr[d2] * 4 + yr[d1] if h == 0 else xr[d1] * 4 + yr[d2]

    own_cols = pl.ds(pl.multiple_of(c * 128, 128), 640)
    gather_w = Gather(M_W, lambda j, lo, n: wall.at[j, pl.ds(lo, n), own_cols], 256, at, message)
    gather_o = Gather(M_WO, lambda j, lo, n: wob.at[j, pl.ds(lo, n), :], 1024, at, message)
    gather_w.own()
    wo_slot = wob.at[dp, pl.ds(pl.multiple_of(c * 512, 512), 512), :]
    sib_wo = message(M_SIB_WO, wo.at[:, pl.ds(pl.multiple_of(other * 128, 128), 128)], wo_slot, sibling)
    sib_wo.start()

    def norm_rows(i, carry):
        rows = pl.ds(pl.multiple_of(i * 16, 16), 16)
        wide = tok[rows, :].astype(F32)
        square = jnp.mean(wide * wide, axis=1, keepdims=True)
        normed = (wide * lax.rsqrt(square + 1e-05) * gain[...]).astype(BF)
        out[rows, :] = normed
        return carry

    lax.fori_loop(0, 8, norm_rows, 0)

    to_home = (order[...] == lax.broadcasted_iota(jnp.int32, (128, 128), 0)).astype(F32)
    to_send = to_home.T.astype(BF)

    def permute(i, carry):
        cols = pl.ds(pl.multiple_of(i * 512, 512), 512)
        for h in range(2):
            src = pl.ds(pl.multiple_of(h * 2048 + i * 512, 512), 512)
            nb[h, :, cols] = jnp.dot(to_send, out[:, src], preferred_element_type=F32).astype(BF)
        return carry

    lax.fori_loop(0, 4, permute, 0)
    sib_rows = message(M_SIB_ROWS, nb.at[other], sib, sibling)
    sib_rows.start()

    column = lax.broadcasted_iota(jnp.int32, (128, 256), 1)
    source = lax.div(column, 16) * 8 + lax.rem(column, 8)
    for h in range(2):
        spread = (lax.broadcasted_iota(jnp.int32, (128, 256), 0) == source) & (lax.rem(lax.div(column, 8), 2) == h)
        pick[h] = jnp.dot(to_home.astype(BF), spread.astype(F32).astype(BF), preferred_element_type=F32).astype(BF)

    sib_rows.wait_recv()

    def interleave(i, carry):
        cols = pl.ds(pl.multiple_of(i * 256, 256), 256)
        mine = nb[c, :, cols].astype(F32)
        his = sib[:, cols].astype(F32)
        low = jnp.where(c == 0, mine, his).reshape(16, 1, 8, 256)
        high = jnp.where(c == 0, his, mine).reshape(16, 1, 8, 256)
        s_buf[:, cols] = jnp.concatenate([low, high], axis=1).reshape(256, 256).astype(BF)
        return carry

    lax.fori_loop(0, 8, interleave, 0)

    def x_rows(half, zz, row, count):
        return x_buf.at[half, pl.ds(pl.multiple_of(zz * 256 + row, 16), count), :]

    def piece(j):
        return s_buf.at[pl.ds(pl.multiple_of(j * 16, 16), 16), :]

    for kx in range(4):
        for ky in range(4):
            if kx or ky:
                j = plane(kx, ky)
                message(M_A2A + kx * 4 + ky, piece(j), x_rows(c, z, dp * 16, 16), (j, sq)).start()
    x_buf[c, pl.ds(pl.multiple_of(z * 256 + dp * 16, 16), 16), :] = s_buf[pl.ds(pl.multiple_of(dp * 16, 16), 16), :]

    def mask_rows(qb, carry):
        seg_q = seg[:, pl.ds(pl.multiple_of(qb * 128, 128), 128)].astype(F32)
        seg_q = jnp.broadcast_to(seg_q, (128, 128)).T
        start = jnp.maximum(qb - 4, 0) * 128
        row_at = qb * 128 + lax.broadcasted_iota(jnp.int32, (128, 128), 0)
        for k in range(5):
            seg_k = seg[:, pl.ds(pl.multiple_of(start + k * 128, 128), 128)].astype(F32)
            col_at = start + k * 128 + lax.broadcasted_iota(jnp.int32, (128, 128), 1)
            visible = (seg_q == seg_k) & (row_at >= col_at)
            bias[qb, :, k * 128 : (k + 1) * 128] = jnp.where(visible, 0.0, NEG)
        return carry

    gather_w.first()
    lax.fori_loop(0, 8, mask_rows, 0)

    def to_sibling(rel, row):
        ref = x_rows(c, zr[rel], row, 64)
        message(M_SIB_X + (rel % 4), ref, ref, sibling).start()

    def arrived(kx):
        for ky in range(4):
            if kx or ky:
                j = plane(-kx if kx == 1 else (1 if kx == 3 else kx), -ky if ky == 1 else (1 if ky == 3 else ky))
                ref = x_rows(c, z, j * 16, 16)
                message(M_A2A + kx * 4 + ky, ref, ref, None).wait_recv()
        row = xr[(4 - kx) % 4] * 64
        ref = x_rows(c, z, row, 64)
        message(M_Z + kx, ref, ref, z_up).start()
        message(M_Z + 4 + kx, ref, ref, z_down).start()
        to_sibling(0, row)

    def passed(kx):
        row = xr[(4 - kx) % 4] * 64
        low = x_rows(c, zr[-1], row, 64)
        message(M_Z + kx, low, low, None).wait_recv()
        if kx % 2 == 0:
            message(M_Z + 8 + kx, low, low, z_up).start()
        to_sibling(-1, row)
        high = x_rows(c, zr[1], row, 64)
        message(M_Z + 4 + kx, high, high, None).wait_recv()
        if kx % 2 == 1:
            message(M_Z + 8 + kx, high, high, z_down).start()
        to_sibling(1, row)

    def opposite(kx):
        row = xr[(4 - kx) % 4] * 64
        ref = x_rows(c, zr[2], row, 64)
        message(M_Z + 8 + kx, ref, ref, None).wait_recv()
        to_sibling(2, row)

    arrived(0)
    arrived(1)
    arrived(2)
    arrived(3)
    gather_w.second()
    passed(0)
    gather_w.third()
    passed(1)
    load_o.wait()
    sib_slot = wob.at[dp, pl.ds(pl.multiple_of(other * 512, 512), 512), :]
    message(M_SIB_WO, sib_slot, sib_slot, None).wait_recv()
    gather_w.last()
    kv_sent = wall.at[:, :, pl.ds(pl.multiple_of(c * 640, 128), 128)]
    kv_came = wall.at[:, :, pl.ds(pl.multiple_of(other * 640, 128), 128)]
    message(M_SIB_KV, kv_sent, kv_sent, sibling).start()
    gather_o.own()
    passed(2)
    passed(3)
    message(M_SIB_KV, kv_came, kv_came, None).wait_recv()

    def project(rel):
        zz = zr[rel]
        ref = x_rows(other, zz, 0, 256)
        message(M_SIB_X + (rel % 4), ref, ref, None).wait_recv()
        rows = pl.ds(pl.multiple_of(zz * 256, 256), 256)

        def columns(n, carry):
            cols = pl.ds(pl.multiple_of(n * 256, 256), 256)
            acc = jnp.dot(x_buf[0, rows, :], wall[0:8, :, cols].reshape(2048, 256), preferred_element_type=F32)
            acc += jnp.dot(x_buf[1, rows, :], wall[8:16, :, cols].reshape(2048, 256), preferred_element_type=F32)
            acc = jnp.transpose(acc.reshape(16, 2, 8, 256), (1, 0, 2, 3)).reshape(256, 256)
            qkv[rows, cols] = acc.astype(BF)
            return carry

        lax.fori_loop(0, 3, columns, 0)

    project(0)
    gather_o.first()
    project(-1)
    gather_o.second()
    project(1)
    for kx in range(4):
        opposite(kx)
    gather_o.third()
    project(2)
    gather_o.last()

    def block(i, carry):
        zz = lax.rem(z + 2 - i + 3 * lax.div(i, 2) - 2 * lax.div(i, 3) + 4, 4)

        def attend(half, carry):
            qb = zz * 2 + half
            rows = pl.ds(pl.multiple_of(qb * 128, 128), 128)
            window = pl.ds(pl.multiple_of(jnp.maximum(qb - 4, 0) * 128, 128), 640)
            query = jnp.concatenate([qkv[rows, 128 + 128 * h : 256 + 128 * h] for h in range(4)], axis=0)
            keys, values = qkv[window, 0:128], qkv[window, 640:768]
            scores = lax.dot_general(query, keys, (((1,), (1,)), ((), ())), preferred_element_type=F32)
            scores = scores.reshape(4, 128, 640) + bias[qb][None]
            top = jnp.max(scores, axis=2, keepdims=True)
            weights = jnp.exp2((scores - top) * EXP_SCALE)
            total = jnp.sum(weights, axis=2, keepdims=True).reshape(512, 1)
            mixed = jnp.dot(weights.astype(BF).reshape(512, 640), values, preferred_element_type=F32) / total
            for h in range(4):
                ho[c, rows, 128 * h : 128 * h + 128] = mixed[128 * h : 128 * h + 128].astype(BF)
            return carry

        lax.fori_loop(0, 2, attend, 0)
        rows = pl.ds(pl.multiple_of(zz * 256, 256), 256)
        message(M_SIB_HO + i, ho.at[c, rows, :], ho.at[c, rows, :], sibling).start()
        message(M_SIB_HO + i, ho.at[other, rows, :], ho.at[other, rows, :], None).wait_recv()

        def columns(n, carry):
            cols = pl.ds(pl.multiple_of(n * 256, 256), 256)
            lhs = jnp.concatenate([ho[0, rows, :], ho[1, rows, :]], axis=1)
            rhs = jnp.concatenate([wob[2 * n], wob[2 * n + 1]], axis=1)
            acc = jnp.dot(lhs, rhs, preferred_element_type=F32)
            acc = jnp.transpose(acc.reshape(2, 16, 8, 256), (1, 0, 2, 3)).reshape(4, 64, 256)
            for xs in range(4):
                kx = lax.rem(xs - x + 4, 4)
                p32[i, kx, :, cols] = acc[xs]
                snd[i, kx, :, cols] = acc[xs].astype(BF)
            return carry

        lax.fori_loop(0, 8, columns, 0)

        @pl.when(i == 0)
        def _():
            for kx in (0, 2, 1, 3):
                message(M_OPP + kx, snd.at[0, kx], opr.at[kx], z_up if kx < 2 else z_down).start()

        @pl.when(i == 1)
        def _():
            for kx in (2, 3):
                message(M_FIN + kx, snd.at[1, kx], fin.at[0, kx], z_up).start()

        @pl.when(i == 2)
        def _():
            for kx in (0, 1):
                message(M_FIN + 4 + kx, snd.at[2, kx], fin.at[1, kx], z_down).start()

        return carry

    lax.fori_loop(0, 4, block, 0)

    for kx in (0, 2, 1, 3):
        side = 0 if kx < 2 else 1
        message(M_OPP + kx, opr.at[kx], opr.at[kx], None).wait_recv()
        snd[1 + side, kx] = (p32[1 + side, kx] + opr[kx].astype(F32)).astype(BF)
        message(M_FIN + 4 * side + kx, snd.at[1 + side, kx], fin.at[side, kx], z_down if side else z_up).start()

    for kx in (0, 2, 1, 3):
        for side in range(2):
            message(M_FIN + 4 * side + kx, fin.at[side, kx], fin.at[side, kx], None).wait_recv()
        for yy in range(4):
            for core in range(2):
                rows = slice(yy * 16 + core * 8, yy * 16 + core * 8 + 8)
                rows2 = slice(yy * 16, yy * 16 + 16)
                tot = p32[3, kx, rows, :]
                for side in range(2):
                    tot = tot + fin[side, kx, rows2, :].astype(F32)[core * 8 : core * 8 + 8]
                fs[kx, yy, core] = jnp.concatenate([tot[:, :1024], tot[:, 1024:]], axis=0).astype(BF)
        for ky in range(4):
            for kc in range(2):
                core = c if kc == 0 else other
                src, dst = fs.at[kx, yr[ky], core], r_buf.at[c, dp]
                if kx or ky or kc:
                    message(M_HOME + kx * 8 + ky * 2 + kc, src, dst, (plane(kx, ky), z * 2 + core)).start()
                else:
                    keep = pltpu.make_async_copy(src, dst, lsem.at[3])
                    keep.start()

    keep.wait()
    for kx in (0, 2, 1, 3):
        for ky in range(4):
            for kc in range(2):
                if kx or ky or kc:
                    j = xr[(4 - kx) % 4] * 4 + yr[(4 - ky) % 4]
                    ref = r_buf.at[c if kc == 0 else other, j]
                    message(M_HOME + kx * 8 + ky * 2 + kc, ref, ref, None).wait_recv()

    for core in range(2):
        for h in range(2):
            back = jnp.dot(pick[h], r_buf[core].reshape(256, 1024), preferred_element_type=F32).astype(BF)
            for i in range(8):
                at_col = (h * 8 + i) * 256 + core * 128
                out[:, at_col : at_col + 128] = back[:, i * 128 : i * 128 + 128]

    sib_rows.wait_send()
    sib_wo.wait_send()
    message(M_SIB_KV, kv_sent, kv_sent, None).wait_send()
    for rel in range(4):
        ref = x_rows(c, zr[rel], 0, 256)
        message(M_SIB_X + rel, ref, ref, None).wait_send()
        ref = ho.at[c, pl.ds(0, 256), :]
        message(M_SIB_HO + rel, ref, ref, None).wait_send()
    for k in range(1, 16):
        message(M_A2A + k, piece(dp), piece(dp), None).wait_send()
    for k in range(12):
        ref = x_rows(c, z, 0, 64)
        message(M_Z + k, ref, ref, None).wait_send()
    gather_w.drain()
    gather_o.drain()
    for kx in range(4):
        message(M_OPP + kx, snd.at[0, kx], opr.at[kx], None).wait_send()
        for side in range(2):
            message(M_FIN + 4 * side + kx, snd.at[1 + side, kx], fin.at[side, kx], None).wait_send()
    for k in range(1, 32):
        message(M_HOME + k, fs.at[0, 0, 0], r_buf.at[0, 0], None).wait_send()


def per_device(tokens, norm_gain, send_order, segment_ids, w_query, w_key, w_value, w_out):
    vmem = pl.BlockSpec(memory_space=pltpu.VMEM)
    hbm = pl.BlockSpec(memory_space=pl.ANY)
    return pl.pallas_call(
        kernel,
        out_shape=jax.ShapeDtypeStruct((128, 4096), BF),
        in_specs=[vmem] * 4 + [hbm] * 4,
        out_specs=vmem,
        scratch_shapes=[
            pltpu.VMEM((2, 1024, 2048), BF),
            pltpu.VMEM((2, 128, 2048), BF),
            pltpu.VMEM((128, 2048), BF),
            pltpu.VMEM((256, 2048), BF),
            pltpu.VMEM((16, 256, 768), BF),
            pltpu.VMEM((16, 1024, 128), BF),
            pltpu.VMEM((1024, 768), BF),
            pltpu.VMEM((2, 1024, 512), BF),
            pltpu.VMEM((8, 128, 640), F32),
            pltpu.VMEM((4, 4, 64, 2048), F32),
            pltpu.VMEM((4, 4, 64, 2048), BF),
            pltpu.VMEM((4, 64, 2048), BF),
            pltpu.VMEM((2, 4, 64, 2048), BF),
            pltpu.VMEM((4, 4, 2, 16, 1024), BF),
            pltpu.VMEM((2, 16, 16, 1024), BF),
            pltpu.VMEM((2, 128, 256), BF),
            pltpu.SemaphoreType.DMA((4,)),
            pltpu.SemaphoreType.DMA((M_COUNT,)),
            pltpu.SemaphoreType.DMA((M_COUNT,)),
        ],
        compiler_params=pltpu.CompilerParams(
            collective_id=0, has_side_effects=True, vmem_limit_bytes=60 * 1024 * 1024
        ),
    )(tokens, norm_gain.reshape(1, 4096), send_order, segment_ids, w_query, w_key, w_value, w_out)


def solution(mesh):
    return jax.shard_map(
        per_device,
        mesh=mesh,
        in_specs=(
            P(("dp", "seq"), None),
            P(),
            P(("dp", "seq"), None),
            P("dp", None),
            P("dp", "seq"),
            P("dp", None),
            P("dp", None),
            P("seq", "dp"),
        ),
        out_specs=P(("dp", "seq"), None),
        check_vma=False,
    )
```

```python
import jax
import jax.numpy as jnp
from jax import lax
from jax.experimental import pallas as pl
from jax.experimental.pallas import tpu as pltpu
from jax.sharding import PartitionSpec as P

BF = jnp.bfloat16
F32 = jnp.float32
MESH = pl.DeviceIdType.MESH
NEG = float("-inf")
EXP_SCALE = 128 ** (-0.5) * 1.4426950408889634

M_SIB_ROWS = 0
M_SIB_WO = 1
M_SIB_KV = 2
M_SIB_X = 3
M_SIB_HO = 7
M_A2A = 11
M_Z = 27
M_W = 75
M_WO = 107
M_OPP = 139
M_FIN = 147
M_HOME = 163
M_COUNT = 195

OFFSETS = (
    (0, 0), (1, 0), (3, 0), (0, 1), (0, 3), (2, 0), (0, 2), (1, 1), (3, 3), (1, 3), (3, 1),
    (2, 1), (2, 3), (1, 2), (3, 2), (2, 2),
)


class Gather:
    PLACE = {
        0: (-1, 0), 1: (1, 0), 2: (2, 0), 3: (2, 0), 4: (0, -1), 5: (-1, -1), 6: (1, -1), 7: (2, -1),
        8: (0, 1), 9: (-1, 1), 10: (1, 1), 11: (2, 1), 12: (0, 2), 13: (-1, 2), 14: (1, 2), 15: (2, 2),
    }
    ONWARD = {
        0: ((2, 1, 0), (5, 0, 1), (9, 0, -1)), 1: ((3, -1, 0), (6, 0, 1), (10, 0, -1)),
        3: ((7, 0, 1), (11, 0, -1)), 4: ((12, 0, 1),), 5: ((13, 0, 1),), 10: ((14, 0, -1),), 11: ((15, 0, -1),),
    }

    def __init__(self, base, view, rows, at, message):
        self.base, self.view, self.rows, self.at, self.message = base, view, rows, at, message

    def part(self, h, d1, d2, quarter=None):
        half = self.rows // 2
        if quarter is None:
            return self.view(self.at(h, d1, d2), h * half, half)
        return self.view(self.at(h, d1, d2), h * half + quarter * (half // 2), half // 2)

    def send(self, h, m, ref, d1, d2):
        self.message(self.base + 16 * h + m, ref, ref, (self.at(h, d1, d2), None)).start()

    def own(self):
        for h in range(2):
            mine = self.part(h, 0, 0)
            self.send(h, 0, mine, 1, 0)
            self.send(h, 1, mine, -1, 0)
            self.send(h, 4, mine, 0, 1)
            self.send(h, 8, mine, 0, -1)

    def take(self, *messages, halves=(0, 1)):
        for m in messages:
            for h in halves:
                d1, d2 = self.PLACE[m]
                ref = self.part(h, d1, d2, m - 2 if m in (2, 3) else None)
                self.message(self.base + 16 * h + m, ref, ref, None).wait_recv()
                for then, s1, s2 in self.ONWARD.get(m, ()):
                    self.send(h, then, self.part(h, d1, d2, then - 2 if then in (2, 3) else None), s1, s2)

    def drain(self):
        for h in range(2):
            for m in range(16):
                ref = self.part(h, 0, 0, 0 if m in (2, 3) else None)
                self.message(self.base + 16 * h + m, ref, ref, None).wait_send()


def kernel(
    tok_hbm, gain, order, seg, wq, wk, wv, wo, out,
    tok, x_buf, nb, sib, s_buf, wall, wob, qkv, ho, bias, p32, snd, opr, fin, fs, r_buf, pick,
    lsem, ssem, rsem,
):
    dp = lax.axis_index("dp")
    sq = lax.axis_index("seq")
    x, y = lax.div(dp, 4), lax.rem(dp, 4)
    z, c = lax.div(sq, 2), lax.rem(sq, 2)
    other = 1 - c

    load_tok = [
        pltpu.make_async_copy(tok_hbm.at[pl.ds(64 * k, 64), :], tok.at[pl.ds(64 * k, 64), :], lsem.at[4 + k])
        for k in range(2)
    ]
    load_tok[0].start()
    load_tok[1].start()

    def ring(v):
        return {0: v, 1: lax.rem(v + 1, 4), 2: lax.rem(v + 2, 4), -1: lax.rem(v + 3, 4), 3: lax.rem(v + 3, 4)}

    xr, yr, zr = ring(x), ring(y), ring(z)

    def plane(kx, ky):
        return xr[kx] * 4 + yr[ky]

    def back(kx, ky):
        return xr[(4 - kx) % 4] * 4 + yr[(4 - ky) % 4]

    def message(index, src, dst, dev):
        if dev is None:
            dev = (dp, z * 2 + other)
        elif dev[1] is None:
            dev = (dev[0], sq)
        return pltpu.make_async_remote_copy(
            src_ref=src, dst_ref=dst, send_sem=ssem.at[index], recv_sem=rsem.at[index],
            device_id=dev, device_id_type=MESH,
        )

    sibling = (dp, z * 2 + other)
    z_up, z_down = (dp, zr[1] * 2 + c), (dp, zr[-1] * 2 + c)

    load_q = pltpu.make_async_copy(wq, wall.at[dp, :, pl.ds(128, 512)], lsem.at[0])
    load_q.start()
    load_o = pltpu.make_async_copy(
        wo.at[:, pl.ds(pl.multiple_of(c * 128, 128), 128)],
        wob.at[dp, pl.ds(pl.multiple_of(c * 512, 512), 512), :], lsem.at[2])
    load_o.start()
    kv_cols = pl.ds(pl.multiple_of(z * 128, 128), 128)
    load_k = pltpu.make_async_copy(wk.at[:, kv_cols], wall.at[dp, :, pl.ds(0, 128)], lsem.at[1])
    load_v = pltpu.make_async_copy(wv.at[:, kv_cols], wall.at[dp, :, pl.ds(640, 128)], lsem.at[1])

    @pl.when(c == 0)
    def _():
        load_k.start()

    @pl.when(c == 1)
    def _():
        load_v.start()

    barrier = pltpu.get_barrier_semaphore()
    greeted = [sibling, z_up, z_down]
    for kx in range(4):
        for ky in range(4):
            if kx or ky:
                greeted.append((plane(kx, ky), sq))
                greeted.append((plane(kx, ky), z * 2 + other))
    for dev in greeted:
        pl.semaphore_signal(barrier, inc=1, device_id=dev, device_id_type=MESH)

    def norm_rows(i, carry):
        rows = pl.ds(pl.multiple_of(i * 16, 16), 16)
        wide = tok[rows, :].astype(F32)
        square = jnp.mean(wide * wide, axis=1, keepdims=True)
        out[rows, :] = (wide * lax.rsqrt(square + 1e-05) * gain[...]).astype(BF)
        return carry

    load_tok[0].wait()
    lax.fori_loop(0, 4, norm_rows, 0)
    load_tok[1].wait()

    @pl.when(c == 0)
    def _():
        load_k.wait()

    @pl.when(c == 1)
    def _():
        load_v.wait()

    load_q.wait()
    pl.semaphore_wait(barrier, len(greeted))

    def at(h, d1, d2):
        return xr[d2] * 4 + yr[d1] if h == 0 else xr[d1] * 4 + yr[d2]

    own_cols = pl.ds(pl.multiple_of(c * 128, 128), 640)
    gather_w = Gather(M_W, lambda j, lo, n: wall.at[j, pl.ds(lo, n), own_cols], 256, at, message)
    gather_o = Gather(M_WO, lambda j, lo, n: wob.at[j, pl.ds(lo, n), :], 1024, at, message)
    gather_w.own()
    lax.fori_loop(4, 8, norm_rows, 0)

    to_home = (order[...] == lax.broadcasted_iota(jnp.int32, (128, 128), 0)).astype(F32)
    to_send = to_home.T.astype(BF)

    def permute(i, carry):
        cols = pl.ds(pl.multiple_of(i * 512, 512), 512)
        nb[carry, :, cols] = jnp.dot(
            to_send, out[:, pl.ds(pl.multiple_of(carry * 2048 + i * 512, 512), 512)], preferred_element_type=F32
        ).astype(BF)
        return carry

    lax.fori_loop(0, 4, permute, other)
    sib_rows = message(M_SIB_ROWS, nb.at[other], sib, sibling)
    sib_rows.start()
    lax.fori_loop(0, 4, permute, c)
    sib_rows.wait_recv()

    def interleave(i, carry):
        cols = pl.ds(pl.multiple_of(i * 256, 256), 256)
        mine = nb[c, :, cols].astype(F32)
        his = sib[:, cols].astype(F32)
        low = jnp.where(c == 0, mine, his).reshape(16, 1, 8, 256)
        high = jnp.where(c == 0, his, mine).reshape(16, 1, 8, 256)
        s_buf[:, cols] = jnp.concatenate([low, high], axis=1).reshape(256, 256).astype(BF)
        return carry

    lax.fori_loop(0, 8, interleave, 0)

    def x_rows(half, zz, row, count):
        return x_buf.at[half, pl.ds(pl.multiple_of(zz * 256 + row, 16), count), :]

    def piece(j):
        return s_buf.at[pl.ds(pl.multiple_of(j * 16, 16), 16), :]

    for kx, ky in OFFSETS[1:]:
        j = plane(kx, ky)
        message(M_A2A + kx * 4 + ky, piece(j), x_rows(c, z, dp * 16, 16), (j, sq)).start()
    x_buf[c, pl.ds(pl.multiple_of(z * 256 + dp * 16, 16), 16), :] = s_buf[pl.ds(pl.multiple_of(dp * 16, 16), 16), :]

    def to_sibling(rel, row):
        ref = x_rows(c, zr[rel], row, 16)
        message(M_SIB_X + (rel % 4), ref, ref, sibling).start()

    def arrived(e):
        kx, ky = OFFSETS[e]
        row = back(kx, ky) * 16
        ref = x_rows(c, z, row, 16)
        if kx or ky:
            message(M_A2A + kx * 4 + ky, ref, ref, None).wait_recv()
        message(M_Z + e, ref, ref, z_up).start()
        message(M_Z + 16 + e, ref, ref, z_down).start()
        to_sibling(0, row)

    def passed(e):
        row = back(*OFFSETS[e]) * 16
        low = x_rows(c, zr[-1], row, 16)
        message(M_Z + e, low, low, None).wait_recv()
        if e % 2 == 0:
            message(M_Z + 32 + e, low, low, z_up).start()
        to_sibling(-1, row)
        high = x_rows(c, zr[1], row, 16)
        message(M_Z + 16 + e, high, high, None).wait_recv()
        if e % 2 == 1:
            message(M_Z + 32 + e, high, high, z_down).start()
        to_sibling(1, row)

    def opposite(e):
        row = back(*OFFSETS[e]) * 16
        ref = x_rows(c, zr[2], row, 16)
        message(M_Z + 32 + e, ref, ref, None).wait_recv()
        to_sibling(2, row)

    arrived(0)
    wo_slot = wob.at[dp, pl.ds(pl.multiple_of(c * 512, 512), 512), :]
    sib_wo = message(M_SIB_WO, wo.at[:, pl.ds(pl.multiple_of(other * 128, 128), 128)], wo_slot, sibling)
    sib_wo.start()
    for e in range(1, 5):
        arrived(e)
    gather_w.take(0, 1)

    def mask_rows(qb, carry):
        seg_q = seg[:, pl.ds(pl.multiple_of(qb * 128, 128), 128)].astype(F32)
        seg_q = jnp.broadcast_to(seg_q, (128, 128)).T
        start = jnp.maximum(qb - 4, 0) * 128
        row_at = qb * 128 + lax.broadcasted_iota(jnp.int32, (128, 128), 0)
        for k in range(5):
            seg_k = seg[:, pl.ds(pl.multiple_of(start + k * 128, 128), 128)].astype(F32)
            col_at = start + k * 128 + lax.broadcasted_iota(jnp.int32, (128, 128), 1)
            visible = (seg_q == seg_k) & (row_at >= col_at)
            bias[qb, :, k * 128 : (k + 1) * 128] = jnp.where(visible, 0.0, NEG)
        return carry

    lax.fori_loop(0, 8, mask_rows, 0)
    for e in range(5, 11):
        arrived(e)
    gather_w.take(4, 8)
    for e in range(11, 16):
        arrived(e)

    column = lax.broadcasted_iota(jnp.int32, (128, 256), 1)
    source = lax.div(column, 16) * 8 + lax.rem(column, 8)
    for h in range(2):
        spread = (lax.broadcasted_iota(jnp.int32, (128, 256), 0) == source) & (lax.rem(lax.div(column, 8), 2) == h)
        pick[h] = jnp.dot(to_home.astype(BF), spread.astype(F32).astype(BF), preferred_element_type=F32).astype(BF)

    gather_w.take(2, 3, 5, 10)
    for e in range(0, 8):
        passed(e)
    gather_w.take(11, 9, 6, 7)
    load_o.wait()
    sib_slot = wob.at[dp, pl.ds(pl.multiple_of(other * 512, 512), 512), :]
    message(M_SIB_WO, sib_slot, sib_slot, None).wait_recv()
    gather_o.own()
    for e in range(8, 16):
        passed(e)
    gather_w.take(12, 13, 14, 15)
    kv_sent = wall.at[:, :, pl.ds(pl.multiple_of(c * 640, 128), 128)]
    kv_came = wall.at[:, :, pl.ds(pl.multiple_of(other * 640, 128), 128)]
    message(M_SIB_KV, kv_sent, kv_sent, sibling).start()
    gather_o.take(0, 1, 4, 8)
    message(M_SIB_KV, kv_came, kv_came, None).wait_recv()

    def project(rel):
        zz = zr[rel]
        ref = x_rows(other, zz, 0, 256)
        message(M_SIB_X + (rel % 4), ref, ref, None).wait_recv()
        rows = pl.ds(pl.multiple_of(zz * 256, 256), 256)

        def columns(n, carry):
            cols = pl.ds(pl.multiple_of(n * 256, 256), 256)
            acc = jnp.dot(x_buf[0, rows, :], wall[0:8, :, cols].reshape(2048, 256), preferred_element_type=F32)
            acc += jnp.dot(x_buf[1, rows, :], wall[8:16, :, cols].reshape(2048, 256), preferred_element_type=F32)
            acc = jnp.transpose(acc.reshape(16, 2, 8, 256), (1, 0, 2, 3)).reshape(256, 256)
            qkv[rows, cols] = acc.astype(BF)
            return carry

        lax.fori_loop(0, 3, columns, 0)

    project(0)
    project(-1)
    gather_o.take(2, 3, 5, 10)
    project(1)
    for e in range(16):
        opposite(e)
    project(2)

    def attend(i, zz):
        def half_block(half, carry):
            qb = zz * 2 + half
            rows = pl.ds(pl.multiple_of(qb * 128, 128), 128)
            window = pl.ds(pl.multiple_of(jnp.maximum(qb - 4, 0) * 128, 128), 640)
            query = jnp.concatenate([qkv[rows, 128 + 128 * h : 256 + 128 * h] for h in range(4)], axis=0)
            keys, values = qkv[window, 0:128], qkv[window, 640:768]
            scores = lax.dot_general(query, keys, (((1,), (1,)), ((), ())), preferred_element_type=F32)
            scores = scores.reshape(4, 128, 640) + bias[qb][None]
            top = jnp.max(scores, axis=2, keepdims=True)
            weights = jnp.exp2((scores - top) * EXP_SCALE)
            total = jnp.sum(weights, axis=2, keepdims=True).reshape(512, 1)
            mixed = jnp.dot(weights.astype(BF).reshape(512, 640), values, preferred_element_type=F32) / total
            for h in range(4):
                ho[c, rows, 128 * h : 128 * h + 128] = mixed[128 * h : 128 * h + 128].astype(BF)
            return carry

        lax.fori_loop(0, 2, half_block, 0)
        rows = pl.ds(pl.multiple_of(zz * 256, 256), 256)
        message(M_SIB_HO + i, ho.at[c, rows, :], ho.at[c, rows, :], sibling).start()

    def project_out(i, zz, xs, half):
        rows = pl.ds(pl.multiple_of(zz * 256, 256), 256)
        cols = pl.ds(pl.multiple_of(xs * 256, 256), 256)
        lhs = jnp.concatenate([ho[0, rows, :], ho[1, rows, :]], axis=1)
        rhs = jnp.concatenate([wob[xs * 4 + half * 2], wob[xs * 4 + half * 2 + 1]], axis=1)
        acc = jnp.dot(lhs, rhs, preferred_element_type=F32)
        acc = jnp.transpose(acc.reshape(2, 16, 8, 256), (1, 0, 2, 3)).reshape(4, 64, 256)
        for row in range(4):
            kx = lax.rem(row - x + 4, 4)
            if i > 0:
                p32[i - 1, kx, half, :, cols] = acc[row]
            if i < 3:
                snd[i, kx, half, :, cols] = acc[row].astype(BF)

    def heads_of_sibling(i, zz):
        ref = ho.at[other, pl.ds(pl.multiple_of(zz * 256, 256), 256), :]
        message(M_SIB_HO + i, ref, ref, None).wait_recv()

    attend(0, zr[2])
    heads_of_sibling(0, zr[2])
    for q, dx in enumerate((0, -1, 1, 2)):
        if q == 0:
            gather_o.take(12, halves=(1,))
        elif q == 1:
            gather_o.take(11)
            gather_o.take(6, 7, halves=(0,))
            gather_o.take(9, 13, halves=(1,))
        elif q == 2:
            gather_o.take(9, halves=(0,))
            gather_o.take(6, 14, halves=(1,))
        else:
            gather_o.take(12, 13, 14, 15, halves=(0,))
            gather_o.take(7, 15, halves=(1,))

        def both(half, carry):
            project_out(0, zr[2], xr[dx], half)
            return carry

        lax.fori_loop(0, 2, both, 0)
        cols = pl.ds(pl.multiple_of(xr[dx] * 256, 256), 256)
        for half, dev in ((0, z_up), (1, z_down)):
            message(M_OPP + 2 * q + half, snd.at[0, :, half, :, cols], opr.at[half, :, :, cols], dev).start()

    def fin_message(side, kx, half):
        return message(
            M_FIN + 8 * side + 2 * kx + half, snd.at[1 + side, kx, half], fin.at[side, kx, half],
            z_down if side else z_up)

    def whole(i, zz):
        attend(i, zz)
        heads_of_sibling(i, zz)

        def both(n, carry):
            project_out(i, zz, lax.div(n, 2), lax.rem(n, 2))
            return carry

        lax.fori_loop(0, 8, both, 0)

    whole(1, zr[1])
    fin_message(0, 0, 1).start()
    fin_message(0, 1, 1).start()
    whole(2, zr[-1])
    fin_message(1, 0, 0).start()
    fin_message(1, 1, 0).start()
    for q, dx in enumerate((0, -1, 1, 2)):
        cols = pl.ds(pl.multiple_of(xr[dx] * 256, 256), 256)
        for half in range(2):
            ref = opr.at[half, :, :, cols]
            message(M_OPP + 2 * q + half, ref, ref, None).wait_recv()
    for kx in range(4):
        for side in range(2):
            snd[1 + side, kx, side] = (p32[side, kx, side] + opr[side, kx].astype(F32)).astype(BF)
            fin_message(side, kx, side).start()
            if kx < 2:
                fin_message(side, kx + 2, 1 - side).start()
    whole(3, z)

    for kx in range(4):
        for side in range(2):
            for half in range(2):
                fin_message(side, kx, half).wait_recv()

        def total(yy, carry):
            rows = pl.ds(pl.multiple_of(yy * 16, 16), 16)
            tot = [
                p32[2, kx, half, rows, :] + fin[0, kx, half, rows, :].astype(F32) + fin[1, kx, half, rows, :].astype(F32)
                for half in range(2)
            ]
            for core in range(2):
                fs[kx, yy, core] = jnp.concatenate([t[core * 8 : core * 8 + 8] for t in tot], axis=0).astype(BF)
            return carry

        lax.fori_loop(0, 4, total, 0)
        for ky in (2, 1, 3, 0):
            for kc in range(2):
                core = c if kc == 0 else other
                src, dst = fs.at[kx, yr[ky], core], r_buf.at[c, dp]
                if kx or ky or kc:
                    message(M_HOME + kx * 8 + ky * 2 + kc, src, dst, (plane(kx, ky), z * 2 + core)).start()
                else:
                    keep = pltpu.make_async_copy(src, dst, lsem.at[3])
                    keep.start()

    keep.wait()
    for kx in range(4):
        for ky in range(4):
            for kc in range(2):
                if kx or ky or kc:
                    ref = r_buf.at[c if kc == 0 else other, back(kx, ky)]
                    message(M_HOME + kx * 8 + ky * 2 + kc, ref, ref, None).wait_recv()

    for core in range(2):
        for h in range(2):
            rows = jnp.dot(pick[h], r_buf[core].reshape(256, 1024), preferred_element_type=F32).astype(BF)
            for i in range(8):
                at_col = (4 * (i // 2) + 2 * h + i % 2) * 256 + core * 128
                out[:, at_col : at_col + 128] = rows[:, i * 128 : i * 128 + 128]

    sib_rows.wait_send()
    sib_wo.wait_send()
    message(M_SIB_KV, kv_sent, kv_sent, None).wait_send()
    for rel in range(4):
        ref = x_rows(c, zr[rel], 0, 256)
        message(M_SIB_X + rel, ref, ref, None).wait_send()
        ref = ho.at[c, pl.ds(0, 256), :]
        message(M_SIB_HO + rel, ref, ref, None).wait_send()
    for k in range(1, 16):
        message(M_A2A + k, piece(dp), piece(dp), None).wait_send()
    for k in range(48):
        ref = x_rows(c, z, 0, 16)
        message(M_Z + k, ref, ref, None).wait_send()
    gather_w.drain()
    gather_o.drain()
    for k in range(8):
        message(M_OPP + k, snd.at[0, :, 0, :, pl.ds(0, 256)], opr.at[0, :, :, pl.ds(0, 256)], None).wait_send()
    for side in range(2):
        for kx in range(4):
            for half in range(2):
                fin_message(side, kx, half).wait_send()
    for k in range(1, 32):
        message(M_HOME + k, fs.at[0, 0, 0], r_buf.at[0, 0], None).wait_send()


def per_device(tokens, norm_gain, send_order, segment_ids, w_query, w_key, w_value, w_out):
    vmem = pl.BlockSpec(memory_space=pltpu.VMEM)
    hbm = pl.BlockSpec(memory_space=pl.ANY)
    return pl.pallas_call(
        kernel,
        out_shape=jax.ShapeDtypeStruct((128, 4096), BF),
        in_specs=[hbm] + [vmem] * 3 + [hbm] * 4,
        out_specs=vmem,
        scratch_shapes=[
            pltpu.VMEM((128, 4096), BF),
            pltpu.VMEM((2, 1024, 2048), BF),
            pltpu.VMEM((2, 128, 2048), BF),
            pltpu.VMEM((128, 2048), BF),
            pltpu.VMEM((256, 2048), BF),
            pltpu.VMEM((16, 256, 768), BF),
            pltpu.VMEM((16, 1024, 128), BF),
            pltpu.VMEM((1024, 768), BF),
            pltpu.VMEM((2, 1024, 512), BF),
            pltpu.VMEM((8, 128, 640), F32),
            pltpu.VMEM((3, 4, 2, 64, 1024), F32),
            pltpu.VMEM((3, 4, 2, 64, 1024), BF),
            pltpu.VMEM((2, 4, 64, 1024), BF),
            pltpu.VMEM((2, 4, 2, 64, 1024), BF),
            pltpu.VMEM((4, 4, 2, 16, 1024), BF),
            pltpu.VMEM((2, 16, 16, 1024), BF),
            pltpu.VMEM((2, 128, 256), BF),
            pltpu.SemaphoreType.DMA((6,)),
            pltpu.SemaphoreType.DMA((M_COUNT,)),
            pltpu.SemaphoreType.DMA((M_COUNT,)),
        ],
        compiler_params=pltpu.CompilerParams(
            collective_id=0, has_side_effects=True, vmem_limit_bytes=60 * 1024 * 1024
        ),
    )(tokens, norm_gain.reshape(1, 4096), send_order, segment_ids, w_query, w_key, w_value, w_out)


def solution(mesh):
    return jax.shard_map(
        per_device,
        mesh=mesh,
        in_specs=(
            P(("dp", "seq"), None),
            P(),
            P(("dp", "seq"), None),
            P("dp", None),
            P("dp", "seq"),
            P("dp", None),
            P("dp", None),
            P("seq", "dp"),
        ),
        out_specs=P(("dp", "seq"), None),
        check_vma=False,
    )
```

```python
import jax
import jax.numpy as jnp
from jax import lax
from jax.experimental import pallas as pl
from jax.experimental.pallas import tpu as pltpu
from jax.sharding import PartitionSpec as P

BF = jnp.bfloat16
F32 = jnp.float32
MESH = pl.DeviceIdType.MESH
NEG = float("-inf")
EXP_SCALE = 128 ** (-0.5) * 1.4426950408889634

M_SIB_ROWS = 0
M_SIB_WO = 1
M_SIB_KV = 2
M_SIB_X = 6
M_SIB_HO = 10
M_A2A = 18
M_Z = 34
M_W = 82
M_WO = 114
M_OPP = 146
M_FIN = 147
M_HOME = 151
M_COUNT = 152
S_SIB, S_WO_SIB, S_KV, S_X, S_HO, S_A2A, S_Z, S_W, S_WO, S_OPP, S_FIN, S_HOME, S_COUNT = range(13)

OFFSETS = (
    (0, 0), (1, 0), (3, 0), (0, 1), (0, 3), (2, 0), (0, 2), (1, 1), (3, 3), (1, 3), (3, 1),
    (2, 1), (2, 3), (1, 2), (3, 2), (2, 2),
)


class Gather:
    PLACE = {
        0: (-1, 0), 1: (1, 0), 2: (2, 0), 3: (2, 0), 4: (0, -1), 5: (-1, -1), 6: (1, -1), 7: (2, -1),
        8: (0, 1), 9: (-1, 1), 10: (1, 1), 11: (2, 1), 12: (0, 2), 13: (-1, 2), 14: (1, 2), 15: (2, 2),
    }
    ONWARD = {
        0: ((2, 1, 0), (5, 0, 1), (9, 0, -1)), 1: ((3, -1, 0), (6, 0, 1), (10, 0, -1)),
        3: ((7, 0, 1), (11, 0, -1)), 4: ((12, 0, 1),), 5: ((13, 0, 1),), 10: ((14, 0, -1),), 11: ((15, 0, -1),),
    }

    def __init__(self, base, group, view, rows, at, message):
        self.base, self.group, self.view, self.rows, self.at, self.message = base, group, view, rows, at, message

    def part(self, h, d1, d2, quarter=None):
        half = self.rows // 2
        if quarter is None:
            return self.view(self.at(h, d1, d2), h * half, half)
        return self.view(self.at(h, d1, d2), h * half + quarter * (half // 2), half // 2)

    def send(self, h, m, ref, d1, d2):
        self.message(self.base + 16 * h + m, self.group, ref, ref, (self.at(h, d1, d2), None)).start()

    def own(self):
        for h in range(2):
            mine = self.part(h, 0, 0)
            self.send(h, 0, mine, 1, 0)
            self.send(h, 1, mine, -1, 0)
            self.send(h, 4, mine, 0, 1)
            self.send(h, 8, mine, 0, -1)

    def take(self, *messages, halves=(0, 1)):
        for m in messages:
            for h in halves:
                d1, d2 = self.PLACE[m]
                ref = self.part(h, d1, d2, m - 2 if m in (2, 3) else None)
                self.message(self.base + 16 * h + m, self.group, ref, ref, None).wait_recv()
                for then, s1, s2 in self.ONWARD.get(m, ()):
                    self.send(h, then, self.part(h, d1, d2, then - 2 if then in (2, 3) else None), s1, s2)


def kernel(
    tok, gain, order, seg, wq, wk, wv, wo, out,
    x_buf, nb, sib, s_buf, wall, wob, qkv, ho, bias, p32, snd, opr, fin, fs, r_buf, pick, part,
    lsem, ssem, rsem,
):
    dp = lax.axis_index("dp")
    sq = lax.axis_index("seq")
    x, y = lax.div(dp, 4), lax.rem(dp, 4)
    z, c = lax.div(sq, 2), lax.rem(sq, 2)
    other = 1 - c

    def ring(v):
        return {0: v, 1: lax.rem(v + 1, 4), 2: lax.rem(v + 2, 4), -1: lax.rem(v + 3, 4), 3: lax.rem(v + 3, 4)}

    xr, yr, zr = ring(x), ring(y), ring(z)

    def plane(kx, ky):
        return xr[kx] * 4 + yr[ky]

    def back(kx, ky):
        return xr[(4 - kx) % 4] * 4 + yr[(4 - ky) % 4]

    def message(index, group, src, dst, dev):
        if dev is None:
            dev = (dp, z * 2 + other)
        elif dev[1] is None:
            dev = (dev[0], sq)
        return pltpu.make_async_remote_copy(
            src_ref=src, dst_ref=dst, send_sem=ssem.at[group], recv_sem=rsem.at[index],
            device_id=dev, device_id_type=MESH,
        )

    sibling = (dp, z * 2 + other)
    z_up, z_down = (dp, zr[1] * 2 + c), (dp, zr[-1] * 2 + c)

    barrier = pltpu.get_barrier_semaphore()
    greeted = [sibling, z_up, z_down]
    for kx in range(4):
        for ky in range(4):
            if kx or ky:
                greeted.append((plane(kx, ky), sq))
                greeted.append((plane(kx, ky), z * 2 + other))
    for dev in greeted:
        pl.semaphore_signal(barrier, inc=1, device_id=dev, device_id_type=MESH)

    load_q = pltpu.make_async_copy(wq, wall.at[dp, :, pl.ds(128, 512)], lsem.at[0])
    load_q.start()
    load_o = pltpu.make_async_copy(
        wo.at[:, pl.ds(pl.multiple_of(c * 128, 128), 128)],
        wob.at[dp, pl.ds(pl.multiple_of(c * 512, 512), 512), :], lsem.at[2])
    load_o.start()
    kv_cols = pl.ds(pl.multiple_of(z * 128, 128), 128)
    load_k = pltpu.make_async_copy(wk.at[:, kv_cols], wall.at[dp, :, pl.ds(0, 128)], lsem.at[1])
    load_v = pltpu.make_async_copy(wv.at[:, kv_cols], wall.at[dp, :, pl.ds(640, 128)], lsem.at[1])

    @pl.when(c == 0)
    def _():
        load_k.start()

    @pl.when(c == 1)
    def _():
        load_v.start()

    def norm_rows(i, carry):
        rows = pl.ds(pl.multiple_of(i * 16, 16), 16)
        wide = tok[rows, :].astype(F32)
        square = jnp.mean(wide * wide, axis=1, keepdims=True)
        out[rows, :] = (wide * lax.rsqrt(square + 1e-05) * gain[...]).astype(BF)
        return carry

    lax.fori_loop(0, 8, norm_rows, 0)

    to_home = (order[...] == lax.broadcasted_iota(jnp.int32, (128, 128), 0)).astype(F32)
    to_send = to_home.T.astype(BF)

    def permute(i, carry):
        half, k = lax.div(i, 4), lax.rem(i, 4)
        nb[half, :, pl.ds(pl.multiple_of(k * 512, 512), 512)] = jnp.dot(
            to_send, out[:, pl.ds(pl.multiple_of(i * 512, 512), 512)], preferred_element_type=F32
        ).astype(BF)
        return carry

    lax.fori_loop(0, 8, permute, 0)

    column = lax.broadcasted_iota(jnp.int32, (128, 256), 1)
    source = lax.div(column, 16) * 8 + lax.rem(column, 8)
    for h in range(2):
        spread = (lax.broadcasted_iota(jnp.int32, (128, 256), 0) == source) & (lax.rem(lax.div(column, 8), 2) == h)
        pick[h] = jnp.dot(to_home.astype(BF), spread.astype(F32).astype(BF), preferred_element_type=F32).astype(BF)

    def mask_rows(qb, carry):
        seg_q = seg[:, pl.ds(pl.multiple_of(qb * 128, 128), 128)].astype(F32)
        seg_q = jnp.broadcast_to(seg_q, (128, 128)).T
        start = jnp.maximum(qb - 4, 0) * 128
        row_at = qb * 128 + lax.broadcasted_iota(jnp.int32, (128, 128), 0)
        for k in range(5):
            seg_k = seg[:, pl.ds(pl.multiple_of(start + k * 128, 128), 128)].astype(F32)
            col_at = start + k * 128 + lax.broadcasted_iota(jnp.int32, (128, 128), 1)
            visible = (seg_q == seg_k) & (row_at >= col_at)
            bias[qb, :, k * 128 : (k + 1) * 128] = jnp.where(visible, 0.0, NEG)
        return carry

    lax.fori_loop(0, 8, mask_rows, 0)

    @pl.when(c == 0)
    def _():
        load_k.wait()

    @pl.when(c == 1)
    def _():
        load_v.wait()

    load_q.wait()
    pl.semaphore_wait(barrier, len(greeted))

    def at(h, d1, d2):
        return xr[d2] * 4 + yr[d1] if h == 0 else xr[d1] * 4 + yr[d2]

    sib_rows = message(M_SIB_ROWS, S_SIB, nb.at[other], sib, sibling)
    sib_rows.start()
    own_cols = pl.ds(pl.multiple_of(c * 128, 128), 640)
    gather_w = Gather(M_W, S_W, lambda j, lo, n: wall.at[j, pl.ds(lo, n), own_cols], 256, at, message)
    gather_o = Gather(M_WO, S_WO, lambda j, lo, n: wob.at[j, pl.ds(lo, n), :], 1024, at, message)
    gather_w.own()
    sib_rows.wait_recv()

    def interleave(i, carry):
        cols = pl.ds(pl.multiple_of(i * 256, 256), 256)
        mine = nb[c, :, cols].astype(F32)
        his = sib[:, cols].astype(F32)
        low = jnp.where(c == 0, mine, his).reshape(16, 1, 8, 256)
        high = jnp.where(c == 0, his, mine).reshape(16, 1, 8, 256)
        s_buf[:, cols] = jnp.concatenate([low, high], axis=1).reshape(256, 256).astype(BF)
        return carry

    lax.fori_loop(0, 8, interleave, 0)

    def x_rows(half, zz, row, count):
        return x_buf.at[half, pl.ds(pl.multiple_of(zz * 256 + row, 16), count), :]

    def piece(j):
        return s_buf.at[pl.ds(pl.multiple_of(j * 16, 16), 16), :]

    for kx, ky in OFFSETS[1:]:
        j = plane(kx, ky)
        message(M_A2A + kx * 4 + ky, S_A2A, piece(j), x_rows(c, z, dp * 16, 16), (j, sq)).start()
    x_buf[c, pl.ds(pl.multiple_of(z * 256 + dp * 16, 16), 16), :] = s_buf[pl.ds(pl.multiple_of(dp * 16, 16), 16), :]

    def to_sibling(rel, row):
        ref = x_rows(c, zr[rel], row, 16)
        message(M_SIB_X + (rel % 4), S_X, ref, ref, sibling).start()

    def arrived(e):
        kx, ky = OFFSETS[e]
        row = back(kx, ky) * 16
        ref = x_rows(c, z, row, 16)
        if kx or ky:
            message(M_A2A + kx * 4 + ky, S_A2A, ref, ref, None).wait_recv()
        message(M_Z + e, S_Z, ref, ref, z_up).start()
        message(M_Z + 16 + e, S_Z, ref, ref, z_down).start()
        to_sibling(0, row)

    def passed(e):
        row = back(*OFFSETS[e]) * 16
        low = x_rows(c, zr[-1], row, 16)
        message(M_Z + e, S_Z, low, low, None).wait_recv()
        if e % 2 == 0:
            message(M_Z + 32 + e, S_Z, low, low, z_up).start()
        to_sibling(-1, row)
        high = x_rows(c, zr[1], row, 16)
        message(M_Z + 16 + e, S_Z, high, high, None).wait_recv()
        if e % 2 == 1:
            message(M_Z + 32 + e, S_Z, high, high, z_down).start()
        to_sibling(1, row)

    def opposite(e):
        row = back(*OFFSETS[e]) * 16
        ref = x_rows(c, zr[2], row, 16)
        message(M_Z + 32 + e, S_Z, ref, ref, None).wait_recv()
        to_sibling(2, row)

    for e in range(7):
        arrived(e)
    wo_slot = wob.at[dp, pl.ds(pl.multiple_of(c * 512, 512), 512), :]
    sib_wo = message(
        M_SIB_WO, S_WO_SIB, wo.at[:, pl.ds(pl.multiple_of(other * 128, 128), 128)], wo_slot, sibling)
    sib_wo.start()
    gather_w.take(0, 1)
    for e in range(7, 11):
        arrived(e)
    gather_w.take(4, 8)
    for e in range(11, 16):
        arrived(e)
    gather_w.take(2, 3, 5, 10)
    for e in range(16):
        passed(e)
    gather_w.take(11)
    load_o.wait()
    sib_slot = wob.at[dp, pl.ds(pl.multiple_of(other * 512, 512), 512), :]
    message(M_SIB_WO, S_WO_SIB, sib_slot, sib_slot, None).wait_recv()
    gather_o.own()

    CHUNKS = (0, -1, 1, 2)

    def take_chunk(gather, q):
        if q == 0:
            gather.take(12, halves=(1,))
        elif q == 1:
            gather.take(6, 7, halves=(0,))
            gather.take(9, 13, halves=(1,))
        elif q == 2:
            gather.take(9, halves=(0,))
            gather.take(6, 14, halves=(1,))
        else:
            gather.take(12, 13, 14, 15, halves=(0,))
            gather.take(7, 15, halves=(1,))

    def kv_message(q, core):
        blocks = pl.ds(xr[CHUNKS[q]] * 4, 4)
        ref = wall.at[blocks, :, pl.ds(pl.multiple_of(core * 640, 128), 128)]
        return message(M_SIB_KV + q, S_KV, ref, ref, sibling)

    def sibling_rows(rel):
        ref = x_rows(other, zr[rel], 0, 256)
        message(M_SIB_X + (rel % 4), S_X, ref, ref, None).wait_recv()

    def store_qkv(rows, cols, acc):
        qkv[rows, cols] = jnp.transpose(acc.reshape(16, 2, 8, 256), (1, 0, 2, 3)).reshape(256, 256).astype(BF)

    def project_chunk(q):
        kv_message(q, other).wait_recv()
        xs = xr[CHUNKS[q]]
        features = pl.ds(pl.multiple_of(lax.rem(xs, 2) * 1024, 1024), 1024)
        blocks = pl.ds(xs * 4, 4)

        def columns(i, carry):
            k, n = lax.div(i, 3), lax.rem(i, 3)
            zz = lax.rem(z + k + lax.div(k, 2), 4)
            rows, cols = pl.ds(pl.multiple_of(zz * 256, 256), 256), pl.ds(pl.multiple_of(n * 256, 256), 256)
            acc = jnp.dot(
                x_buf[lax.div(xs, 2), rows, features], wall[blocks, :, cols].reshape(1024, 256),
                preferred_element_type=F32)
            if q > 0:
                acc += part[rows, cols]
            if q < 3:
                part[rows, cols] = acc
            else:
                store_qkv(rows, cols, acc)
            return carry

        lax.fori_loop(0, 9, columns, 0)

    take_chunk(gather_w, 0)
    kv_message(0, c).start()
    sibling_rows(0)
    sibling_rows(-1)
    sibling_rows(1)
    take_chunk(gather_w, 1)
    kv_message(1, c).start()
    project_chunk(0)
    take_chunk(gather_w, 2)
    kv_message(2, c).start()
    project_chunk(1)
    take_chunk(gather_w, 3)
    kv_message(3, c).start()
    project_chunk(2)
    for e in range(8):
        opposite(e)
    gather_o.take(0, 1, 4, 8)
    project_chunk(3)
    for e in range(8, 16):
        opposite(e)

    def project(rel):
        sibling_rows(rel)
        rows = pl.ds(pl.multiple_of(zr[rel] * 256, 256), 256)

        def columns(n, carry):
            cols = pl.ds(pl.multiple_of(n * 256, 256), 256)
            acc = jnp.dot(x_buf[0, rows, :], wall[0:8, :, cols].reshape(2048, 256), preferred_element_type=F32)
            acc += jnp.dot(x_buf[1, rows, :], wall[8:16, :, cols].reshape(2048, 256), preferred_element_type=F32)
            store_qkv(rows, cols, acc)
            return carry

        lax.fori_loop(0, 3, columns, 0)

    gather_o.take(2, 3)
    project(2)
    gather_o.take(5, 10)

    def attend(i, zz):
        def half_block(half, carry):
            qb = zz * 2 + half
            rows = pl.ds(pl.multiple_of(qb * 128, 128), 128)
            window = pl.ds(pl.multiple_of(jnp.maximum(qb - 4, 0) * 128, 128), 640)
            query = jnp.concatenate([qkv[rows, 128 + 128 * h : 256 + 128 * h] for h in range(4)], axis=0)
            keys, values = qkv[window, 0:128], qkv[window, 640:768]
            scores = lax.dot_general(query, keys, (((1,), (1,)), ((), ())), preferred_element_type=F32)
            scores = scores.reshape(4, 128, 640) + bias[qb][None]
            top = jnp.max(scores, axis=2, keepdims=True)
            weights = jnp.exp2((scores - top) * EXP_SCALE)
            total = jnp.sum(weights, axis=2, keepdims=True).reshape(512, 1)
            mixed = jnp.dot(weights.astype(BF).reshape(512, 640), values, preferred_element_type=F32) / total
            for h in range(4):
                ho[c, rows, 128 * h : 128 * h + 128] = mixed[128 * h : 128 * h + 128].astype(BF)
            message(M_SIB_HO + 2 * i + half, S_HO, ho.at[c, rows, :], ho.at[c, rows, :], sibling).start()
            return carry

        lax.fori_loop(0, 2, half_block, 0)

    def project_out(i, zz, xs, half):
        rows = pl.ds(pl.multiple_of(zz * 256, 256), 256)
        cols = pl.ds(pl.multiple_of(xs * 256, 256), 256)
        lhs = jnp.concatenate([ho[0, rows, :], ho[1, rows, :]], axis=1)
        rhs = jnp.concatenate([wob[xs * 4 + half * 2], wob[xs * 4 + half * 2 + 1]], axis=1)
        acc = jnp.dot(lhs, rhs, preferred_element_type=F32)
        acc = jnp.transpose(acc.reshape(2, 16, 8, 256), (1, 0, 2, 3)).reshape(4, 64, 256)
        for row in range(4):
            kx = lax.rem(row - x + 4, 4)
            if i > 0:
                p32[i - 1, kx, half, :, cols] = acc[row]
            if i < 3:
                snd[i, kx, half, :, cols] = acc[row].astype(BF)

    def heads_of_sibling(i, zz):
        for half in range(2):
            ref = ho.at[other, pl.ds(pl.multiple_of(zz * 256 + half * 128, 128), 128), :]
            message(M_SIB_HO + 2 * i + half, S_HO, ref, ref, None).wait_recv()

    def farthest(q):
        if q == 1:
            gather_o.take(11)
        take_chunk(gather_o, q)
        xs = xr[CHUNKS[q]]

        def both(half, carry):
            project_out(0, zr[2], xs, half)
            return carry

        lax.fori_loop(0, 2, both, 0)
        cols = pl.ds(pl.multiple_of(xs * 256, 256), 256)
        for half, dev in ((0, z_up), (1, z_down)):
            message(M_OPP, S_OPP, snd.at[0, :, half, :, cols], opr.at[half, :, :, cols], dev).start()

    def fin_message(side, kx, half):
        return message(
            M_FIN + kx, S_FIN, snd.at[1 + side, kx, half], fin.at[kx, side, half], z_down if side else z_up)

    def project_whole(i, zz):
        heads_of_sibling(i, zz)

        def both(n, carry):
            project_out(i, zz, lax.div(n, 2), lax.rem(n, 2))
            return carry

        lax.fori_loop(0, 8, both, 0)

    attend(0, zr[2])
    heads_of_sibling(0, zr[2])
    farthest(0)
    attend(1, zr[1])
    farthest(1)
    attend(2, zr[-1])
    farthest(2)
    farthest(3)
    project_whole(1, zr[1])
    fin_message(0, 0, 1).start()
    fin_message(0, 1, 1).start()
    project_whole(2, zr[-1])
    fin_message(1, 0, 0).start()
    fin_message(1, 1, 0).start()
    message(M_OPP, S_OPP, opr, opr, None).wait_recv()
    for kx in range(4):
        for side in range(2):
            snd[1 + side, kx, side] = (p32[side, kx, side] + opr[side, kx].astype(F32)).astype(BF)
            fin_message(side, kx, side).start()
            if kx < 2:
                fin_message(side, kx + 2, 1 - side).start()
    attend(3, z)
    project_whole(3, z)

    for kx in range(4):
        message(M_FIN + kx, S_FIN, fin.at[kx], fin.at[kx], None).wait_recv()

        def total(yy, carry):
            rows = pl.ds(pl.multiple_of(yy * 16, 16), 16)
            tot = [
                p32[2, kx, half, rows, :] + fin[kx, 0, half, rows, :].astype(F32) + fin[kx, 1, half, rows, :].astype(F32)
                for half in range(2)
            ]
            for core in range(2):
                fs[kx * 8 + yy * 2 + core] = jnp.concatenate([t[core * 8 : core * 8 + 8] for t in tot], axis=0).astype(BF)
            return carry

        lax.fori_loop(0, 4, total, 0)
        for ky in (2, 1, 3, 0):
            for kc in range(2):
                core = c if kc == 0 else other
                src, dst = fs.at[kx * 8 + yr[ky] * 2 + core], r_buf.at[c * 16 + dp]
                if kx or ky or kc:
                    message(M_HOME, S_HOME, src, dst, (plane(kx, ky), z * 2 + core)).start()
                else:
                    keep = pltpu.make_async_copy(src, dst, lsem.at[3])
                    keep.start()

    keep.wait()
    came = r_buf.at[pl.ds(0, 31)]
    message(M_HOME, S_HOME, came, came, None).wait_recv()

    for core in range(2):
        for h in range(2):
            rows = jnp.dot(pick[h], r_buf[core * 16 : core * 16 + 16].reshape(256, 1024), preferred_element_type=F32).astype(BF)
            for i in range(8):
                at_col = (4 * (i // 2) + 2 * h + i % 2) * 256 + core * 128
                out[:, at_col : at_col + 128] = rows[:, i * 128 : i * 128 + 128]

    def sent(group, ref):
        message(0, group, ref, ref, None).wait_send()

    sent(S_SIB, sib)
    sent(S_WO_SIB, wo_slot)
    sent(S_KV, wall.at[:, :, pl.ds(0, 128)])
    sent(S_X, x_buf.at[0])
    sent(S_HO, ho.at[0])
    sent(S_A2A, s_buf.at[pl.ds(0, 240), :])
    sent(S_Z, x_buf.at[0, pl.ds(0, 768), :])
    sent(S_W, wall.at[pl.ds(0, 15), :, pl.ds(0, 640)])
    sent(S_WO, wob.at[pl.ds(0, 15)])
    sent(S_OPP, snd.at[0])
    sent(S_FIN, snd.at[pl.ds(1, 2)])
    sent(S_HOME, fs.at[pl.ds(0, 31)])


def per_device(tokens, norm_gain, send_order, segment_ids, w_query, w_key, w_value, w_out):
    vmem = pl.BlockSpec(memory_space=pltpu.VMEM)
    hbm = pl.BlockSpec(memory_space=pl.ANY)
    return pl.pallas_call(
        kernel,
        out_shape=jax.ShapeDtypeStruct((128, 4096), BF),
        in_specs=[vmem] * 4 + [hbm] * 4,
        out_specs=vmem,
        scratch_shapes=[
            pltpu.VMEM((2, 1024, 2048), BF),
            pltpu.VMEM((2, 128, 2048), BF),
            pltpu.VMEM((128, 2048), BF),
            pltpu.VMEM((256, 2048), BF),
            pltpu.VMEM((16, 256, 768), BF),
            pltpu.VMEM((16, 1024, 128), BF),
            pltpu.VMEM((1024, 768), BF),
            pltpu.VMEM((2, 1024, 512), BF),
            pltpu.VMEM((8, 128, 640), F32),
            pltpu.VMEM((3, 4, 2, 64, 1024), F32),
            pltpu.VMEM((3, 4, 2, 64, 1024), BF),
            pltpu.VMEM((2, 4, 64, 1024), BF),
            pltpu.VMEM((4, 2, 2, 64, 1024), BF),
            pltpu.VMEM((32, 16, 1024), BF),
            pltpu.VMEM((32, 16, 1024), BF),
            pltpu.VMEM((2, 128, 256), BF),
            pltpu.VMEM((1024, 768), F32),
            pltpu.SemaphoreType.DMA((4,)),
            pltpu.SemaphoreType.DMA((S_COUNT,)),
            pltpu.SemaphoreType.DMA((M_COUNT,)),
        ],
        compiler_params=pltpu.CompilerParams(
            collective_id=0, has_side_effects=True, vmem_limit_bytes=60 * 1024 * 1024
        ),
    )(tokens, norm_gain.reshape(1, 4096), send_order, segment_ids, w_query, w_key, w_value, w_out)


def solution(mesh):
    return jax.shard_map(
        per_device,
        mesh=mesh,
        in_specs=(
            P(("dp", "seq"), None),
            P(),
            P(("dp", "seq"), None),
            P("dp", None),
            P("dp", "seq"),
            P("dp", None),
            P("dp", None),
            P("seq", "dp"),
        ),
        out_specs=P(("dp", "seq"), None),
        check_vma=False,
    )
```

```python
import jax
import jax.numpy as jnp
from jax import lax
from jax.experimental import pallas as pl
from jax.experimental.pallas import tpu as pltpu
from jax.sharding import PartitionSpec as P

BF = jnp.bfloat16
F32 = jnp.float32
MESH = pl.DeviceIdType.MESH
NEG = float("-inf")
EXP_SCALE = 128 ** (-0.5) * 1.4426950408889634

M_SIB_ROWS = 0
M_SIB_WO = 1
M_SIB_KV = 2
M_SIB_X = 6
M_SIB_HO = 10
M_A2A = 18
M_Z = 34
M_W = 82
M_WO = 114
M_OPP = 146
M_FIN = 147
M_HOME = 151
M_COUNT = 152
S_SIB, S_WO_SIB, S_KV, S_X, S_HO, S_A2A, S_Z, S_W, S_WO, S_OPP, S_FIN, S_HOME, S_COUNT = range(13)

OFFSETS = (
    (0, 0), (1, 0), (3, 0), (0, 1), (0, 3), (2, 0), (0, 2), (1, 1), (3, 3), (1, 3), (3, 1),
    (2, 1), (2, 3), (1, 2), (3, 2), (2, 2),
)


class Gather:
    PLACE = {
        0: (-1, 0), 1: (1, 0), 2: (2, 0), 3: (2, 0), 4: (0, -1), 5: (-1, -1), 6: (1, -1), 7: (2, -1),
        8: (0, 1), 9: (-1, 1), 10: (1, 1), 11: (2, 1), 12: (0, 2), 13: (-1, 2), 14: (1, 2), 15: (2, 2),
    }
    ONWARD = {
        0: ((2, 1, 0), (5, 0, 1), (9, 0, -1)), 1: ((3, -1, 0), (6, 0, 1), (10, 0, -1)),
        3: ((7, 0, 1), (11, 0, -1)), 4: ((12, 0, 1),), 5: ((13, 0, 1),), 10: ((14, 0, -1),), 11: ((15, 0, -1),),
    }

    def __init__(self, base, group, view, rows, at, message):
        self.base, self.group, self.view, self.rows, self.at, self.message = base, group, view, rows, at, message

    def part(self, h, d1, d2, quarter=None):
        half = self.rows // 2
        if quarter is None:
            return self.view(self.at(h, d1, d2), h * half, half)
        return self.view(self.at(h, d1, d2), h * half + quarter * (half // 2), half // 2)

    def send(self, h, m, ref, d1, d2):
        self.message(self.base + 16 * h + m, self.group, ref, ref, (self.at(h, d1, d2), None)).start()

    def own(self):
        for h in range(2):
            mine = self.part(h, 0, 0)
            self.send(h, 0, mine, 1, 0)
            self.send(h, 1, mine, -1, 0)
            self.send(h, 4, mine, 0, 1)
            self.send(h, 8, mine, 0, -1)

    def take(self, *messages, halves=(0, 1)):
        for m in messages:
            for h in halves:
                d1, d2 = self.PLACE[m]
                ref = self.part(h, d1, d2, m - 2 if m in (2, 3) else None)
                self.message(self.base + 16 * h + m, self.group, ref, ref, None).wait_recv()
                for then, s1, s2 in self.ONWARD.get(m, ()):
                    self.send(h, then, self.part(h, d1, d2, then - 2 if then in (2, 3) else None), s1, s2)


def kernel(
    tok, gain, order, seg, wq, wk, wv, wo, out,
    x_buf, nb, sib, s_buf, wall, wob, qkv, ho, bias, p32, snd, opr, fin, fs, r_buf, pick, part,
    lsem, ssem, rsem,
):
    dp = lax.axis_index("dp")
    sq = lax.axis_index("seq")
    x, y = lax.div(dp, 4), lax.rem(dp, 4)
    z, c = lax.div(sq, 2), lax.rem(sq, 2)
    other = 1 - c

    def ring(v):
        return {0: v, 1: lax.rem(v + 1, 4), 2: lax.rem(v + 2, 4), -1: lax.rem(v + 3, 4), 3: lax.rem(v + 3, 4)}

    xr, yr, zr = ring(x), ring(y), ring(z)

    def plane(kx, ky):
        return xr[kx] * 4 + yr[ky]

    def back(kx, ky):
        return xr[(4 - kx) % 4] * 4 + yr[(4 - ky) % 4]

    def message(index, group, src, dst, dev):
        if dev is None:
            dev = (dp, z * 2 + other)
        elif dev[1] is None:
            dev = (dev[0], sq)
        return pltpu.make_async_remote_copy(
            src_ref=src, dst_ref=dst, send_sem=ssem.at[group], recv_sem=rsem.at[index],
            device_id=dev, device_id_type=MESH,
        )

    sibling = (dp, z * 2 + other)
    z_up, z_down = (dp, zr[1] * 2 + c), (dp, zr[-1] * 2 + c)

    barrier = pltpu.get_barrier_semaphore()
    greeted = [sibling, z_up, z_down]
    for kx in range(4):
        for ky in range(4):
            if kx or ky:
                greeted.append((plane(kx, ky), sq))
                greeted.append((plane(kx, ky), z * 2 + other))
    for dev in greeted:
        pl.semaphore_signal(barrier, inc=1, device_id=dev, device_id_type=MESH)

    load_q = pltpu.make_async_copy(wq, wall.at[dp, :, pl.ds(128, 512)], lsem.at[0])
    load_q.start()
    load_o = pltpu.make_async_copy(
        wo.at[:, pl.ds(pl.multiple_of(c * 128, 128), 128)],
        wob.at[dp, pl.ds(pl.multiple_of(c * 512, 512), 512), :], lsem.at[2])
    load_o.start()
    kv_cols = pl.ds(pl.multiple_of(z * 128, 128), 128)
    load_k = pltpu.make_async_copy(wk.at[:, kv_cols], wall.at[dp, :, pl.ds(0, 128)], lsem.at[1])
    load_v = pltpu.make_async_copy(wv.at[:, kv_cols], wall.at[dp, :, pl.ds(640, 128)], lsem.at[1])

    @pl.when(c == 0)
    def _():
        load_k.start()

    @pl.when(c == 1)
    def _():
        load_v.start()

    def norm_rows(i, carry):
        rows = pl.ds(pl.multiple_of(i * 16, 16), 16)
        wide = tok[rows, :].astype(F32)
        square = jnp.mean(wide * wide, axis=1, keepdims=True)
        out[rows, :] = (wide * lax.rsqrt(square + 1e-05) * gain[...]).astype(BF)
        return carry

    lax.fori_loop(0, 8, norm_rows, 0)

    to_home = (order[...] == lax.broadcasted_iota(jnp.int32, (128, 128), 0)).astype(F32)
    to_send = to_home.T.astype(BF)

    def permute(i, carry):
        half, k = lax.div(i, 4), lax.rem(i, 4)
        nb[half, :, pl.ds(pl.multiple_of(k * 512, 512), 512)] = jnp.dot(
            to_send, out[:, pl.ds(pl.multiple_of(i * 512, 512), 512)], preferred_element_type=F32
        ).astype(BF)
        return carry

    lax.fori_loop(0, 8, permute, 0)

    column = lax.broadcasted_iota(jnp.int32, (128, 256), 1)
    source = lax.div(column, 16) * 8 + lax.rem(column, 8)
    for h in range(2):
        spread = (lax.broadcasted_iota(jnp.int32, (128, 256), 0) == source) & (lax.rem(lax.div(column, 8), 2) == h)
        pick[h] = jnp.dot(to_home.astype(BF), spread.astype(F32).astype(BF), preferred_element_type=F32).astype(BF)

    def mask_rows(qb, carry):
        seg_q = seg[:, pl.ds(pl.multiple_of(qb * 128, 128), 128)].astype(F32)
        seg_q = jnp.broadcast_to(seg_q, (128, 128)).T
        start = jnp.maximum(qb - 4, 0) * 128
        row_at = qb * 128 + lax.broadcasted_iota(jnp.int32, (128, 128), 0)
        for k in range(5):
            seg_k = seg[:, pl.ds(pl.multiple_of(start + k * 128, 128), 128)].astype(F32)
            col_at = start + k * 128 + lax.broadcasted_iota(jnp.int32, (128, 128), 1)
            visible = (seg_q == seg_k) & (row_at >= col_at)
            bias[qb, :, k * 128 : (k + 1) * 128] = jnp.where(visible, 0.0, NEG)
        return carry

    lax.fori_loop(0, 8, mask_rows, 0)

    @pl.when(c == 0)
    def _():
        load_k.wait()

    @pl.when(c == 1)
    def _():
        load_v.wait()

    load_q.wait()
    pl.semaphore_wait(barrier, len(greeted))

    def at(h, d1, d2):
        return xr[d2] * 4 + yr[d1] if h == 0 else xr[d1] * 4 + yr[d2]

    sib_rows = message(M_SIB_ROWS, S_SIB, nb.at[other], sib, sibling)
    sib_rows.start()
    own_cols = pl.ds(pl.multiple_of(c * 128, 128), 640)
    gather_w = Gather(M_W, S_W, lambda j, lo, n: wall.at[j, pl.ds(lo, n), own_cols], 256, at, message)
    gather_o = Gather(M_WO, S_WO, lambda j, lo, n: wob.at[j, pl.ds(lo, n), :], 1024, at, message)
    sib_rows.wait_recv()

    def interleave(i, carry):
        cols = pl.ds(pl.multiple_of(i * 256, 256), 256)
        mine = nb[c, :, cols].astype(F32)
        his = sib[:, cols].astype(F32)
        low = jnp.where(c == 0, mine, his).reshape(16, 1, 8, 256)
        high = jnp.where(c == 0, his, mine).reshape(16, 1, 8, 256)
        s_buf[:, cols] = jnp.concatenate([low, high], axis=1).reshape(256, 256).astype(BF)
        return carry

    lax.fori_loop(0, 8, interleave, 0)

    def x_rows(half, zz, row, count):
        return x_buf.at[half, pl.ds(pl.multiple_of(zz * 256 + row, 16), count), :]

    def piece(j):
        return s_buf.at[pl.ds(pl.multiple_of(j * 16, 16), 16), :]

    def scatter(first, last):
        for kx, ky in OFFSETS[first:last]:
            j = plane(kx, ky)
            message(M_A2A + kx * 4 + ky, S_A2A, piece(j), x_rows(c, z, dp * 16, 16), (j, sq)).start()

    scatter(1, 7)
    x_buf[c, pl.ds(pl.multiple_of(z * 256 + dp * 16, 16), 16), :] = s_buf[pl.ds(pl.multiple_of(dp * 16, 16), 16), :]

    def to_sibling(rel, row):
        ref = x_rows(c, zr[rel], row, 16)
        message(M_SIB_X + (rel % 4), S_X, ref, ref, sibling).start()

    def arrived(e):
        kx, ky = OFFSETS[e]
        row = back(kx, ky) * 16
        ref = x_rows(c, z, row, 16)
        if kx or ky:
            message(M_A2A + kx * 4 + ky, S_A2A, ref, ref, None).wait_recv()
        message(M_Z + e, S_Z, ref, ref, z_up).start()
        message(M_Z + 16 + e, S_Z, ref, ref, z_down).start()
        to_sibling(0, row)

    def passed(e):
        row = back(*OFFSETS[e]) * 16
        low = x_rows(c, zr[-1], row, 16)
        message(M_Z + e, S_Z, low, low, None).wait_recv()
        if e % 2 == 0:
            message(M_Z + 32 + e, S_Z, low, low, z_up).start()
        to_sibling(-1, row)
        high = x_rows(c, zr[1], row, 16)
        message(M_Z + 16 + e, S_Z, high, high, None).wait_recv()
        if e % 2 == 1:
            message(M_Z + 32 + e, S_Z, high, high, z_down).start()
        to_sibling(1, row)

    def opposite(e):
        row = back(*OFFSETS[e]) * 16
        ref = x_rows(c, zr[2], row, 16)
        message(M_Z + 32 + e, S_Z, ref, ref, None).wait_recv()
        to_sibling(2, row)

    arrived(0)
    gather_w.own()
    for e in range(1, 5):
        arrived(e)
    scatter(7, 11)
    wo_slot = wob.at[dp, pl.ds(pl.multiple_of(c * 512, 512), 512), :]
    sib_wo = message(
        M_SIB_WO, S_WO_SIB, wo.at[:, pl.ds(pl.multiple_of(other * 128, 128), 128)], wo_slot, sibling)
    sib_wo.start()
    for e in range(5, 7):
        arrived(e)
    scatter(11, 16)
    gather_w.take(0, 1)
    for e in range(7, 11):
        arrived(e)
    gather_w.take(4, 8)
    for e in range(11, 16):
        arrived(e)

    GROUPS = (
        ((0, 0), (0, 1), (0, -1), (1, 0), (-1, 0)),
        ((0, 2), (2, 0), (1, 1), (1, -1), (-1, 1), (-1, -1)),
        ((2, 1), (2, -1), (1, 2), (-1, 2), (2, 2)),
    )

    def kv_send(q):
        cols = pl.ds(pl.multiple_of(c * 640, 128), 128)
        for kx, ky in GROUPS[q]:
            ref = wall.at[plane(kx, ky), :, cols]
            message(M_SIB_KV + q, S_KV, ref, ref, sibling).start()

    def kv_wait(q):
        ref = wall.at[pl.ds(0, len(GROUPS[q])), :, pl.ds(pl.multiple_of(other * 640, 128), 128)]
        message(M_SIB_KV + q, S_KV, ref, ref, None).wait_recv()

    def sibling_rows(rel):
        ref = x_rows(other, zr[rel], 0, 256)
        message(M_SIB_X + (rel % 4), S_X, ref, ref, None).wait_recv()

    def project(q, first, last):
        blocks = [plane(kx, ky) for kx, ky in GROUPS[q]]

        def columns(i, carry):
            k, n = lax.div(i, 3), lax.rem(i, 3)
            zz = lax.rem(z + k + lax.div(k, 2) - 2 * lax.div(k, 3), 4)
            rows, cols = pl.ds(pl.multiple_of(zz * 256, 256), 256), pl.ds(pl.multiple_of(n * 256, 256), 256)
            acc = part[rows, cols] if q > 0 else 0.0
            for j in blocks:
                features = pl.ds(pl.multiple_of(lax.rem(j, 8) * 256, 256), 256)
                acc += jnp.dot(x_buf[lax.div(j, 8), rows, features], wall[j, :, cols], preferred_element_type=F32)
            if q < 2:
                part[rows, cols] = acc
            else:
                acc = jnp.transpose(acc.reshape(16, 2, 8, 256), (1, 0, 2, 3)).reshape(256, 256)
                qkv[rows, cols] = acc.astype(BF)
            return carry

        lax.fori_loop(3 * first, 3 * last, columns, 0)

    gather_w.take(2, 3, 5, 10)
    kv_send(0)
    for e in range(8):
        passed(e)
    sibling_rows(0)
    kv_wait(0)
    project(0, 0, 1)
    for e in range(8, 16):
        passed(e)
    gather_w.take(12, 6, 9, 11)
    kv_send(1)
    load_o.wait()
    sib_slot = wob.at[dp, pl.ds(pl.multiple_of(other * 512, 512), 512), :]
    message(M_SIB_WO, S_WO_SIB, sib_slot, sib_slot, None).wait_recv()
    gather_o.own()
    sibling_rows(1)
    sibling_rows(-1)
    project(0, 1, 3)
    kv_wait(1)
    project(1, 0, 3)
    for e in range(16):
        opposite(e)
    gather_w.take(7, 13, 14, 15)
    kv_send(2)
    sibling_rows(2)
    project(0, 3, 4)
    project(1, 3, 4)
    kv_wait(2)
    gather_o.take(0, 1, 4, 8)
    project(2, 0, 4)
    gather_o.take(2, 3, 5, 10)

    CHUNKS = (0, -1, 1, 2)

    def take_chunk(gather, q):
        if q == 0:
            gather.take(12, halves=(1,))
        elif q == 1:
            gather.take(6, 7, halves=(0,))
            gather.take(9, 13, halves=(1,))
        elif q == 2:
            gather.take(9, halves=(0,))
            gather.take(6, 14, halves=(1,))
        else:
            gather.take(12, 13, 14, 15, halves=(0,))
            gather.take(7, 15, halves=(1,))

    def attend(i, zz):
        def half_block(half, carry):
            qb = zz * 2 + half
            rows = pl.ds(pl.multiple_of(qb * 128, 128), 128)
            window = pl.ds(pl.multiple_of(jnp.maximum(qb - 4, 0) * 128, 128), 640)
            query = jnp.concatenate([qkv[rows, 128 + 128 * h : 256 + 128 * h] for h in range(4)], axis=0)
            keys, values = qkv[window, 0:128], qkv[window, 640:768]
            scores = lax.dot_general(query, keys, (((1,), (1,)), ((), ())), preferred_element_type=F32)
            scores = scores.reshape(4, 128, 640) + bias[qb][None]
            top = jnp.max(scores, axis=2, keepdims=True)
            weights = jnp.exp2((scores - top) * EXP_SCALE)
            total = jnp.sum(weights, axis=2, keepdims=True).reshape(512, 1)
            mixed = jnp.dot(weights.astype(BF).reshape(512, 640), values, preferred_element_type=F32) / total
            for h in range(4):
                ho[c, rows, 128 * h : 128 * h + 128] = mixed[128 * h : 128 * h + 128].astype(BF)
            message(M_SIB_HO + 2 * i + half, S_HO, ho.at[c, rows, :], ho.at[c, rows, :], sibling).start()
            return carry

        lax.fori_loop(0, 2, half_block, 0)

    def project_out(i, zz, xs, half):
        rows = pl.ds(pl.multiple_of(zz * 256, 256), 256)
        cols = pl.ds(pl.multiple_of(xs * 256, 256), 256)
        lhs = jnp.concatenate([ho[0, rows, :], ho[1, rows, :]], axis=1)
        rhs = jnp.concatenate([wob[xs * 4 + half * 2], wob[xs * 4 + half * 2 + 1]], axis=1)
        acc = jnp.dot(lhs, rhs, preferred_element_type=F32)
        acc = jnp.transpose(acc.reshape(2, 16, 8, 256), (1, 0, 2, 3)).reshape(16, 16, 256)
        for j in range(16):
            kx, ky = lax.rem(j // 4 - x + 4, 4), lax.rem(j % 4 - y + 4, 4)
            group, at_row = lax.rem(ky - kx + 4, 4), pl.ds(pl.multiple_of(kx * 16, 16), 16)
            if i > 0:
                p32[i - 1, group, half, at_row, cols] = acc[j]
            if i < 3:
                snd[i, group, half, at_row, cols] = acc[j].astype(BF)

    def heads_of_sibling(i, zz):
        for half in range(2):
            ref = ho.at[other, pl.ds(pl.multiple_of(zz * 256 + half * 128, 128), 128), :]
            message(M_SIB_HO + 2 * i + half, S_HO, ref, ref, None).wait_recv()

    def farthest(q):
        if q == 1:
            gather_o.take(11)
        take_chunk(gather_o, q)
        xs = xr[CHUNKS[q]]

        def both(half, carry):
            project_out(0, zr[2], xs, half)
            return carry

        lax.fori_loop(0, 2, both, 0)
        cols = pl.ds(pl.multiple_of(xs * 256, 256), 256)
        for half, dev in ((0, z_up), (1, z_down)):
            message(M_OPP, S_OPP, snd.at[0, :, half, :, cols], opr.at[half, :, :, cols], dev).start()

    def fin_message(side, group, half):
        return message(
            M_FIN + group, S_FIN, snd.at[1 + side, group, half], fin.at[group, side, half],
            z_down if side else z_up)

    def project_whole(i, zz):
        heads_of_sibling(i, zz)

        def both(n, carry):
            project_out(i, zz, lax.div(n, 2), lax.rem(n, 2))
            return carry

        lax.fori_loop(0, 8, both, 0)

    attend(0, zr[2])
    heads_of_sibling(0, zr[2])
    farthest(0)
    attend(1, zr[1])
    farthest(1)
    attend(2, zr[-1])
    farthest(2)
    farthest(3)
    project_whole(1, zr[1])
    fin_message(0, 0, 1).start()
    fin_message(0, 1, 1).start()
    project_whole(2, zr[-1])
    fin_message(1, 0, 0).start()
    fin_message(1, 1, 0).start()
    message(M_OPP, S_OPP, opr, opr, None).wait_recv()
    for group in range(4):
        for side in range(2):
            snd[1 + side, group, side] = (p32[side, group, side] + opr[side, group].astype(F32)).astype(BF)
            fin_message(side, group, side).start()
            if group < 2:
                fin_message(side, group + 2, 1 - side).start()
    attend(3, z)
    project_whole(3, z)

    for group in range(4):
        message(M_FIN + group, S_FIN, fin.at[group], fin.at[group], None).wait_recv()

        def total(k, carry):
            rows = pl.ds(pl.multiple_of(k * 16, 16), 16)
            tot = [
                p32[2, group, half, rows, :] + fin[group, 0, half, rows, :].astype(F32)
                + fin[group, 1, half, rows, :].astype(F32)
                for half in range(2)
            ]
            for core in range(2):
                fs[group * 8 + k * 2 + core] = jnp.concatenate(
                    [t[core * 8 : core * 8 + 8] for t in tot], axis=0).astype(BF)
            return carry

        lax.fori_loop(0, 4, total, 0)
        for k in (2, 1, 3, 0):
            for same in range(2):
                core = other if same == 0 else c
                src, dst = fs.at[group * 8 + k * 2 + core], r_buf.at[c * 16 + dp]
                if group or k or same == 0:
                    message(M_HOME, S_HOME, src, dst, (plane(k, (k + group) % 4), z * 2 + core)).start()
                else:
                    keep = pltpu.make_async_copy(src, dst, lsem.at[3])
                    keep.start()

    keep.wait()
    came = r_buf.at[pl.ds(0, 31)]
    message(M_HOME, S_HOME, came, came, None).wait_recv()

    for core in range(2):
        for h in range(2):
            rows = jnp.dot(pick[h], r_buf[core * 16 : core * 16 + 16].reshape(256, 1024), preferred_element_type=F32).astype(BF)
            for i in range(8):
                at_col = (4 * (i // 2) + 2 * h + i % 2) * 256 + core * 128
                out[:, at_col : at_col + 128] = rows[:, i * 128 : i * 128 + 128]

    def sent(group, ref):
        message(0, group, ref, ref, None).wait_send()

    sent(S_SIB, sib)
    sent(S_WO_SIB, wo_slot)
    sent(S_KV, wall.at[:, :, pl.ds(0, 128)])
    sent(S_X, x_buf.at[0])
    sent(S_HO, ho.at[0])
    sent(S_A2A, s_buf.at[pl.ds(0, 240), :])
    sent(S_Z, x_buf.at[0, pl.ds(0, 768), :])
    sent(S_W, wall.at[pl.ds(0, 15), :, pl.ds(0, 640)])
    sent(S_WO, wob.at[pl.ds(0, 15)])
    sent(S_OPP, snd.at[0])
    sent(S_FIN, snd.at[pl.ds(1, 2)])
    sent(S_HOME, fs.at[pl.ds(0, 31)])


def per_device(tokens, norm_gain, send_order, segment_ids, w_query, w_key, w_value, w_out):
    vmem = pl.BlockSpec(memory_space=pltpu.VMEM)
    hbm = pl.BlockSpec(memory_space=pl.ANY)
    return pl.pallas_call(
        kernel,
        out_shape=jax.ShapeDtypeStruct((128, 4096), BF),
        in_specs=[vmem] * 4 + [hbm] * 4,
        out_specs=vmem,
        scratch_shapes=[
            pltpu.VMEM((2, 1024, 2048), BF),
            pltpu.VMEM((2, 128, 2048), BF),
            pltpu.VMEM((128, 2048), BF),
            pltpu.VMEM((256, 2048), BF),
            pltpu.VMEM((16, 256, 768), BF),
            pltpu.VMEM((16, 1024, 128), BF),
            pltpu.VMEM((1024, 768), BF),
            pltpu.VMEM((2, 1024, 512), BF),
            pltpu.VMEM((8, 128, 640), F32),
            pltpu.VMEM((3, 4, 2, 64, 1024), F32),
            pltpu.VMEM((3, 4, 2, 64, 1024), BF),
            pltpu.VMEM((2, 4, 64, 1024), BF),
            pltpu.VMEM((4, 2, 2, 64, 1024), BF),
            pltpu.VMEM((32, 16, 1024), BF),
            pltpu.VMEM((32, 16, 1024), BF),
            pltpu.VMEM((2, 128, 256), BF),
            pltpu.VMEM((1024, 768), F32),
            pltpu.SemaphoreType.DMA((4,)),
            pltpu.SemaphoreType.DMA((S_COUNT,)),
            pltpu.SemaphoreType.DMA((M_COUNT,)),
        ],
        compiler_params=pltpu.CompilerParams(
            collective_id=0, has_side_effects=True, vmem_limit_bytes=60 * 1024 * 1024
        ),
    )(tokens, norm_gain.reshape(1, 4096), send_order, segment_ids, w_query, w_key, w_value, w_out)


def solution(mesh):
    return jax.shard_map(
        per_device,
        mesh=mesh,
        in_specs=(
            P(("dp", "seq"), None),
            P(),
            P(("dp", "seq"), None),
            P("dp", None),
            P("dp", "seq"),
            P("dp", None),
            P("dp", None),
            P("seq", "dp"),
        ),
        out_specs=P(("dp", "seq"), None),
        check_vma=False,
    )
```

```python
import jax
import jax.numpy as jnp
from jax import lax
from jax.experimental import pallas as pl
from jax.experimental.pallas import tpu as pltpu
from jax.sharding import PartitionSpec as P

BF = jnp.bfloat16
F32 = jnp.float32
MESH = pl.DeviceIdType.MESH
NEG = float("-inf")
EXP_SCALE = 128 ** (-0.5) * 1.4426950408889634

M_SIB_ROWS = 0
M_SIB_WO = 1
M_SIB_KV = 2
M_SIB_X = 6
M_SIB_HO = 10
M_A2A = 18
M_Z = 34
M_W = 82
M_WO = 114
M_OPP = 146
M_FIN = 147
M_HOME = 151
M_COUNT = 152
S_SIB, S_WO_SIB, S_KV, S_X, S_HO, S_A2A, S_Z, S_W, S_WO, S_OPP, S_FIN, S_HOME, S_COUNT = range(13)

OFFSETS = (
    (0, 0), (1, 0), (3, 0), (0, 1), (0, 3), (2, 0), (0, 2), (1, 1), (3, 3), (1, 3), (3, 1),
    (2, 1), (2, 3), (1, 2), (3, 2), (2, 2),
)


class Gather:
    PLACE = {
        0: (-1, 0), 1: (1, 0), 2: (2, 0), 3: (2, 0), 4: (0, -1), 5: (-1, -1), 6: (1, -1), 7: (2, -1),
        8: (0, 1), 9: (-1, 1), 10: (1, 1), 11: (2, 1), 12: (0, 2), 13: (-1, 2), 14: (1, 2), 15: (2, 2),
    }
    ONWARD = {
        0: ((2, 1, 0), (5, 0, 1), (9, 0, -1)), 1: ((3, -1, 0), (6, 0, 1), (10, 0, -1)),
        3: ((7, 0, 1), (11, 0, -1)), 4: ((12, 0, 1),), 5: ((13, 0, 1),), 10: ((14, 0, -1),), 11: ((15, 0, -1),),
    }

    def __init__(self, base, group, view, rows, at, message):
        self.base, self.group, self.view, self.rows, self.at, self.message = base, group, view, rows, at, message

    def part(self, h, d1, d2, quarter=None):
        half = self.rows // 2
        if quarter is None:
            return self.view(self.at(h, d1, d2), h * half, half)
        return self.view(self.at(h, d1, d2), h * half + quarter * (half // 2), half // 2)

    def send(self, h, m, ref, d1, d2):
        self.message(self.base + 16 * h + m, self.group, ref, ref, (self.at(h, d1, d2), None)).start()

    def own(self, halves=(0, 1)):
        for h in halves:
            mine = self.part(h, 0, 0)
            self.send(h, 0, mine, 1, 0)
            self.send(h, 1, mine, -1, 0)
            self.send(h, 4, mine, 0, 1)
            self.send(h, 8, mine, 0, -1)

    def take(self, *messages, halves=(0, 1)):
        for m in messages:
            for h in halves:
                d1, d2 = self.PLACE[m]
                ref = self.part(h, d1, d2, m - 2 if m in (2, 3) else None)
                self.message(self.base + 16 * h + m, self.group, ref, ref, None).wait_recv()
                for then, s1, s2 in self.ONWARD.get(m, ()):
                    self.send(h, then, self.part(h, d1, d2, then - 2 if then in (2, 3) else None), s1, s2)


def kernel(
    tok, gain, order, seg, wq, wk, wv, wo, out,
    x_buf, nb, sib, s_buf, wall, wob, qkv, ho, bias, p32, snd, opr, fin, fs, r_buf, pick, part,
    lsem, ssem, rsem,
):
    dp = lax.axis_index("dp")
    sq = lax.axis_index("seq")
    x, y = lax.div(dp, 4), lax.rem(dp, 4)
    z, c = lax.div(sq, 2), lax.rem(sq, 2)
    other = 1 - c

    def ring(v):
        return {0: v, 1: lax.rem(v + 1, 4), 2: lax.rem(v + 2, 4), -1: lax.rem(v + 3, 4), 3: lax.rem(v + 3, 4)}

    xr, yr, zr = ring(x), ring(y), ring(z)

    def plane(kx, ky):
        return xr[kx] * 4 + yr[ky]

    def back(kx, ky):
        return xr[(4 - kx) % 4] * 4 + yr[(4 - ky) % 4]

    def half_of(kx, ky):
        return lax.div(lax.rem(ky + 3 * lax.div(kx, 2), 4), 2)

    def message(index, group, src, dst, dev):
        if dev is None:
            dev = (dp, z * 2 + other)
        elif dev[1] is None:
            dev = (dev[0], sq)
        return pltpu.make_async_remote_copy(
            src_ref=src, dst_ref=dst, send_sem=ssem.at[group], recv_sem=rsem.at[index],
            device_id=dev, device_id_type=MESH,
        )

    sibling = (dp, z * 2 + other)
    z_up, z_down = (dp, zr[1] * 2 + c), (dp, zr[-1] * 2 + c)

    barrier = pltpu.get_barrier_semaphore()
    greeted = [sibling, z_up, z_down]
    for kx in range(4):
        for ky in range(4):
            if kx or ky:
                greeted.append((plane(kx, ky), sq))
                greeted.append((plane(kx, ky), z * 2 + other))
    for dev in greeted:
        pl.semaphore_signal(barrier, inc=1, device_id=dev, device_id_type=MESH)

    load_q = pltpu.make_async_copy(wq, wall.at[dp, :, pl.ds(128, 512)], lsem.at[0])
    load_q.start()
    load_o = pltpu.make_async_copy(
        wo.at[:, pl.ds(pl.multiple_of(c * 128, 128), 128)],
        wob.at[dp, pl.ds(pl.multiple_of(c * 512, 512), 512), :], lsem.at[2])
    load_o.start()
    kv_cols = pl.ds(pl.multiple_of(z * 128, 128), 128)
    load_k = pltpu.make_async_copy(wk.at[:, kv_cols], wall.at[dp, :, pl.ds(0, 128)], lsem.at[1])
    load_v = pltpu.make_async_copy(wv.at[:, kv_cols], wall.at[dp, :, pl.ds(640, 128)], lsem.at[1])

    @pl.when(c == 0)
    def _():
        load_k.start()

    @pl.when(c == 1)
    def _():
        load_v.start()

    def norm_rows(i, carry):
        rows = pl.ds(pl.multiple_of(i * 16, 16), 16)
        wide = tok[rows, :].astype(F32)
        square = jnp.mean(wide * wide, axis=1, keepdims=True)
        out[rows, :] = (wide * lax.rsqrt(square + 1e-05) * gain[...]).astype(BF)
        return carry

    lax.fori_loop(0, 8, norm_rows, 0)

    to_home = (order[...] == lax.broadcasted_iota(jnp.int32, (128, 128), 0)).astype(F32)
    to_send = to_home.T.astype(BF)

    def permute(i, carry):
        half, k = lax.div(i, 4), lax.rem(i, 4)
        nb[half, :, pl.ds(pl.multiple_of(k * 512, 512), 512)] = jnp.dot(
            to_send, out[:, pl.ds(pl.multiple_of(i * 512, 512), 512)], preferred_element_type=F32
        ).astype(BF)
        return carry

    lax.fori_loop(0, 8, permute, 0)

    column = lax.broadcasted_iota(jnp.int32, (128, 256), 1)
    source = lax.div(column, 16) * 8 + lax.rem(column, 8)
    spread = lax.broadcasted_iota(jnp.int32, (128, 256), 0) == source
    whence = jnp.dot(to_home.astype(BF), spread.astype(F32).astype(BF), preferred_element_type=F32)
    group_x, group_y = lax.div(column, 64), lax.rem(lax.div(column, 16), 4)
    piece_half = lax.rem(lax.div(column, 8), 2)

    def pick_block(j, carry):
        here = half_of(lax.rem(lax.div(j, 4) - group_x + 4, 4), lax.rem(lax.rem(j, 4) - group_y + 4, 4))
        pick[j] = jnp.where(here == piece_half, whence, 0.0).astype(BF)
        return carry

    lax.fori_loop(0, 16, pick_block, 0)

    def mask_rows(qb, carry):
        seg_q = seg[:, pl.ds(pl.multiple_of(qb * 128, 128), 128)].astype(F32)
        seg_q = jnp.broadcast_to(seg_q, (128, 128)).T
        start = jnp.maximum(qb - 4, 0) * 128
        row_at = qb * 128 + lax.broadcasted_iota(jnp.int32, (128, 128), 0)
        for k in range(5):
            seg_k = seg[:, pl.ds(pl.multiple_of(start + k * 128, 128), 128)].astype(F32)
            col_at = start + k * 128 + lax.broadcasted_iota(jnp.int32, (128, 128), 1)
            visible = (seg_q == seg_k) & (row_at >= col_at)
            bias[qb, :, k * 128 : (k + 1) * 128] = jnp.where(visible, 0.0, NEG)
        return carry

    lax.fori_loop(0, 8, mask_rows, 0)

    @pl.when(c == 0)
    def _():
        load_k.wait()

    @pl.when(c == 1)
    def _():
        load_v.wait()

    load_q.wait()
    pl.semaphore_wait(barrier, len(greeted))

    def at(h, d1, d2):
        return xr[d2] * 4 + yr[d1] if h == 0 else xr[d1] * 4 + yr[d2]

    sib_rows = message(M_SIB_ROWS, S_SIB, nb.at[other], sib, sibling)
    sib_rows.start()
    own_cols = pl.ds(pl.multiple_of(c * 128, 128), 640)
    gather_w = Gather(M_W, S_W, lambda j, lo, n: wall.at[j, pl.ds(lo, n), own_cols], 256, at, message)
    gather_o = Gather(M_WO, S_WO, lambda j, lo, n: wob.at[j, pl.ds(lo, n), :], 1024, at, message)
    gather_w.own(halves=(0,))
    sib_rows.wait_recv()

    def interleave(i, carry):
        cols = pl.ds(pl.multiple_of(i * 256, 256), 256)
        mine = nb[c, :, cols].astype(F32)
        his = sib[:, cols].astype(F32)
        low = jnp.where(c == 0, mine, his).reshape(16, 1, 8, 256)
        high = jnp.where(c == 0, his, mine).reshape(16, 1, 8, 256)
        s_buf[:, cols] = jnp.concatenate([low, high], axis=1).reshape(256, 256).astype(BF)
        return carry

    lax.fori_loop(0, 8, interleave, 0)

    def x_rows(half, zz, row, count):
        return x_buf.at[half, pl.ds(pl.multiple_of(zz * 256 + row, 16), count), :]

    def piece(j):
        return s_buf.at[pl.ds(pl.multiple_of(j * 16, 16), 16), :]

    def scatter(first, last):
        for kx, ky in OFFSETS[first:last]:
            j = plane(kx, ky)
            message(M_A2A + kx * 4 + ky, S_A2A, piece(j), x_rows(c, z, dp * 16, 16), (j, sq)).start()

    scatter(1, 7)
    x_buf[c, pl.ds(pl.multiple_of(z * 256 + dp * 16, 16), 16), :] = s_buf[pl.ds(pl.multiple_of(dp * 16, 16), 16), :]

    def to_sibling(rel, row):
        ref = x_rows(c, zr[rel], row, 16)
        message(M_SIB_X + (rel % 4), S_X, ref, ref, sibling).start()

    def arrived(e):
        kx, ky = OFFSETS[e]
        row = back(kx, ky) * 16
        ref = x_rows(c, z, row, 16)
        if kx or ky:
            message(M_A2A + kx * 4 + ky, S_A2A, ref, ref, None).wait_recv()
        message(M_Z + e, S_Z, ref, ref, z_up).start()
        message(M_Z + 16 + e, S_Z, ref, ref, z_down).start()
        to_sibling(0, row)

    def passed(e):
        row = back(*OFFSETS[e]) * 16
        low = x_rows(c, zr[-1], row, 16)
        message(M_Z + e, S_Z, low, low, None).wait_recv()
        if e % 2 == 0:
            message(M_Z + 32 + e, S_Z, low, low, z_up).start()
        to_sibling(-1, row)
        high = x_rows(c, zr[1], row, 16)
        message(M_Z + 16 + e, S_Z, high, high, None).wait_recv()
        if e % 2 == 1:
            message(M_Z + 32 + e, S_Z, high, high, z_down).start()
        to_sibling(1, row)

    def opposite(e):
        row = back(*OFFSETS[e]) * 16
        ref = x_rows(c, zr[2], row, 16)
        message(M_Z + 32 + e, S_Z, ref, ref, None).wait_recv()
        to_sibling(2, row)

    arrived(0)
    gather_w.own(halves=(1,))
    for e in range(1, 5):
        arrived(e)
    scatter(7, 11)
    wo_slot = wob.at[dp, pl.ds(pl.multiple_of(c * 512, 512), 512), :]
    sib_wo = message(
        M_SIB_WO, S_WO_SIB, wo.at[:, pl.ds(pl.multiple_of(other * 128, 128), 128)], wo_slot, sibling)
    sib_wo.start()
    for e in range(5, 7):
        arrived(e)
    scatter(11, 16)
    gather_w.take(0, 1)
    for e in range(7, 11):
        arrived(e)
    gather_w.take(4, 8)
    for e in range(11, 16):
        arrived(e)

    GROUPS = (
        ((0, 0), (0, 1), (0, -1), (1, 0), (-1, 0)),
        ((0, 2), (2, 0), (1, 1), (1, -1), (-1, 1), (-1, -1)),
        ((2, 1), (2, -1), (1, 2), (-1, 2), (2, 2)),
    )

    def kv_send(q):
        cols = pl.ds(pl.multiple_of(c * 640, 128), 128)
        for kx, ky in GROUPS[q]:
            ref = wall.at[plane(kx, ky), :, cols]
            message(M_SIB_KV + q, S_KV, ref, ref, sibling).start()

    def kv_wait(q):
        ref = wall.at[pl.ds(0, len(GROUPS[q])), :, pl.ds(pl.multiple_of(other * 640, 128), 128)]
        message(M_SIB_KV + q, S_KV, ref, ref, None).wait_recv()

    def sibling_rows(rel):
        ref = x_rows(other, zr[rel], 0, 256)
        message(M_SIB_X + (rel % 4), S_X, ref, ref, None).wait_recv()

    def project(q, first, last):
        blocks = [plane(kx, ky) for kx, ky in GROUPS[q]]

        def columns(i, carry):
            k, n = lax.div(i, 3), lax.rem(i, 3)
            zz = lax.rem(z + k + lax.div(k, 2) - 2 * lax.div(k, 3), 4)
            rows, cols = pl.ds(pl.multiple_of(zz * 256, 256), 256), pl.ds(pl.multiple_of(n * 256, 256), 256)
            acc = part[rows, cols] if q > 0 else 0.0
            for j in blocks:
                features = pl.ds(pl.multiple_of(lax.rem(j, 8) * 256, 256), 256)
                acc += jnp.dot(x_buf[lax.div(j, 8), rows, features], wall[j, :, cols], preferred_element_type=F32)
            if q < 2:
                part[rows, cols] = acc
            else:
                acc = jnp.transpose(acc.reshape(16, 2, 8, 256), (1, 0, 2, 3)).reshape(256, 256)
                qkv[rows, cols] = acc.astype(BF)
            return carry

        lax.fori_loop(3 * first, 3 * last, columns, 0)

    gather_w.take(2, 3, 5, 10)
    kv_send(0)
    for e in range(8):
        passed(e)
    sibling_rows(0)
    kv_wait(0)
    project(0, 0, 1)
    for e in range(8, 16):
        passed(e)
    gather_w.take(12, 6, 9, 11)
    kv_send(1)
    load_o.wait()
    sib_slot = wob.at[dp, pl.ds(pl.multiple_of(other * 512, 512), 512), :]
    message(M_SIB_WO, S_WO_SIB, sib_slot, sib_slot, None).wait_recv()
    gather_o.own()
    sibling_rows(1)
    sibling_rows(-1)
    project(0, 1, 3)
    kv_wait(1)
    project(1, 0, 3)
    for e in range(16):
        opposite(e)
    sibling_rows(2)
    project(0, 3, 4)
    project(1, 3, 4)
    gather_w.take(7, 13, 14, 15)
    kv_send(2)
    gather_o.take(0, 1, 4, 8)
    kv_wait(2)
    project(2, 0, 4)
    gather_o.take(2, 3, 5, 10)

    def attend(i, zz):
        def half_block(half, carry):
            qb = zz * 2 + half
            rows = pl.ds(pl.multiple_of(qb * 128, 128), 128)
            window = pl.ds(pl.multiple_of(jnp.maximum(qb - 4, 0) * 128, 128), 640)
            query = jnp.concatenate([qkv[rows, 128 + 128 * h : 256 + 128 * h] for h in range(4)], axis=0)
            keys, values = qkv[window, 0:128], qkv[window, 640:768]
            scores = lax.dot_general(query, keys, (((1,), (1,)), ((), ())), preferred_element_type=F32)
            scores = scores.reshape(4, 128, 640) + bias[qb][None]
            top = jnp.max(scores, axis=2, keepdims=True)
            weights = jnp.exp2((scores - top) * EXP_SCALE)
            total = jnp.sum(weights, axis=2, keepdims=True).reshape(512, 1)
            mixed = jnp.dot(weights.astype(BF).reshape(512, 640), values, preferred_element_type=F32) / total
            for h in range(4):
                ho[c, rows, 128 * h : 128 * h + 128] = mixed[128 * h : 128 * h + 128].astype(BF)
            message(M_SIB_HO + 2 * i + half, S_HO, ho.at[c, rows, :], ho.at[c, rows, :], sibling).start()
            return carry

        lax.fori_loop(0, 2, half_block, 0)

    def project_out(i, zz, blocks):
        rows = pl.ds(pl.multiple_of(zz * 256, 256), 256)
        lhs = jnp.concatenate([ho[0, rows, :], ho[1, rows, :]], axis=1)
        rhs = [wob[j] for j in blocks]
        acc = jnp.dot(lhs, rhs[0] if len(rhs) == 1 else jnp.concatenate(rhs, axis=1), preferred_element_type=F32)
        acc = jnp.transpose(acc.reshape(2, 16, 8, 128 * len(blocks)), (1, 0, 2, 3)).reshape(16, 16, 128 * len(blocks))
        for n, j in enumerate(blocks):
            bx, by = lax.div(j, 4), lax.rem(j, 4)
            half = half_of(lax.rem(bx - x + 4, 4), lax.rem(by - y + 4, 4))
            cols = pl.ds(pl.multiple_of((bx * 2 + lax.rem(by, 2)) * 128, 128), 128)
            for at_j in range(16):
                kx, ky = lax.rem(at_j // 4 - x + 4, 4), lax.rem(at_j % 4 - y + 4, 4)
                group, at_row = lax.rem(ky - kx + 4, 4), pl.ds(pl.multiple_of(kx * 16, 16), 16)
                val = acc[at_j, :, 128 * n : 128 * n + 128]
                if i > 0:
                    p32[i - 1, group, half, at_row, cols] = val
                if i < 3:
                    snd[i, group, half, at_row, cols] = val.astype(BF)

    def heads_of_sibling(i, zz):
        for half in range(2):
            ref = ho.at[other, pl.ds(pl.multiple_of(zz * 256 + half * 128, 128), 128), :]
            message(M_SIB_HO + 2 * i + half, S_HO, ref, ref, None).wait_recv()

    HALF = lambda kx, ky: ((ky % 4 + 3 * (kx % 4 // 2)) % 4) // 2

    def farthest(q):
        offsets = GROUPS[q]
        for first in range(0, len(offsets), 2):
            project_out(0, zr[2], [plane(kx, ky) for kx, ky in offsets[first : first + 2]])
            for kx, ky in offsets[first : first + 2]:
                half, place = HALF(kx, ky), xr[kx] * 2 + lax.rem(yr[ky], 2)
                cols = pl.ds(pl.multiple_of(place * 128, 128), 128)
                message(
                    M_OPP, S_OPP, snd.at[0, :, half, :, cols], opr.at[half, :, :, cols],
                    z_down if half else z_up).start()

    def fin_message(side, group, half):
        return message(
            M_FIN + group, S_FIN, snd.at[1 + side, group, half], fin.at[group, side, half],
            z_down if side else z_up)

    def project_whole(i, zz):
        heads_of_sibling(i, zz)

        def both(n, carry):
            j = lax.div(n, 2) * 4 + lax.rem(n, 2)
            project_out(i, zz, [j, j + 2])
            return carry

        lax.fori_loop(0, 8, both, 0)

    attend(0, zr[2])
    heads_of_sibling(0, zr[2])
    farthest(0)
    gather_o.take(12, 6, 9)
    farthest(1)
    gather_o.take(11)
    attend(1, zr[1])
    gather_o.take(7, 13, 14, 15)
    farthest(2)
    attend(2, zr[-1])
    project_whole(1, zr[1])
    fin_message(0, 0, 1).start()
    fin_message(0, 1, 1).start()
    project_whole(2, zr[-1])
    fin_message(1, 0, 0).start()
    fin_message(1, 1, 0).start()
    message(M_OPP, S_OPP, opr, opr, None).wait_recv()
    for group in range(4):
        for side in range(2):
            snd[1 + side, group, side] = (p32[side, group, side] + opr[side, group].astype(F32)).astype(BF)
            fin_message(side, group, side).start()
            if group < 2:
                fin_message(side, group + 2, 1 - side).start()
    attend(3, z)
    project_whole(3, z)

    for group in range(4):
        message(M_FIN + group, S_FIN, fin.at[group], fin.at[group], None).wait_recv()

        def total(k, carry):
            rows = pl.ds(pl.multiple_of(k * 16, 16), 16)
            tot = [
                p32[2, group, half, rows, :] + fin[group, 0, half, rows, :].astype(F32)
                + fin[group, 1, half, rows, :].astype(F32)
                for half in range(2)
            ]
            for core in range(2):
                fs[group * 8 + k * 2 + core] = jnp.concatenate(
                    [t[core * 8 : core * 8 + 8] for t in tot], axis=0).astype(BF)
            return carry

        lax.fori_loop(0, 4, total, 0)
        for k in (2, 1, 3, 0):
            for same in range(2):
                core = other if same == 0 else c
                src, dst = fs.at[group * 8 + k * 2 + core], r_buf.at[c * 16 + dp]
                if group or k or same == 0:
                    message(M_HOME, S_HOME, src, dst, (plane(k, (k + group) % 4), z * 2 + core)).start()
                else:
                    keep = pltpu.make_async_copy(src, dst, lsem.at[3])
                    keep.start()

    keep.wait()
    came = r_buf.at[pl.ds(0, 31)]
    message(M_HOME, S_HOME, came, came, None).wait_recv()

    for j in range(16):
        place = (j // 4) * 2 + j % 2
        cols = slice(place * 128, place * 128 + 128)
        rhs = jnp.concatenate([r_buf[16 * core : 16 * core + 16, :, cols].reshape(256, 128) for core in range(2)], axis=1)
        out[:, j * 256 : j * 256 + 256] = jnp.dot(pick[j], rhs, preferred_element_type=F32).astype(BF)

    def sent(group, ref):
        message(0, group, ref, ref, None).wait_send()

    sent(S_SIB, sib)
    sent(S_WO_SIB, wo_slot)
    sent(S_KV, wall.at[:, :, pl.ds(0, 128)])
    sent(S_X, x_buf.at[0])
    sent(S_HO, ho.at[0])
    sent(S_A2A, s_buf.at[pl.ds(0, 240), :])
    sent(S_Z, x_buf.at[0, pl.ds(0, 768), :])
    sent(S_W, wall.at[pl.ds(0, 15), :, pl.ds(0, 640)])
    sent(S_WO, wob.at[pl.ds(0, 15)])
    sent(S_OPP, snd.at[0])
    sent(S_FIN, snd.at[pl.ds(1, 2)])
    sent(S_HOME, fs.at[pl.ds(0, 31)])


def per_device(tokens, norm_gain, send_order, segment_ids, w_query, w_key, w_value, w_out):
    vmem = pl.BlockSpec(memory_space=pltpu.VMEM)
    hbm = pl.BlockSpec(memory_space=pl.ANY)
    return pl.pallas_call(
        kernel,
        out_shape=jax.ShapeDtypeStruct((128, 4096), BF),
        in_specs=[vmem] * 4 + [hbm] * 4,
        out_specs=vmem,
        scratch_shapes=[
            pltpu.VMEM((2, 1024, 2048), BF),
            pltpu.VMEM((2, 128, 2048), BF),
            pltpu.VMEM((128, 2048), BF),
            pltpu.VMEM((256, 2048), BF),
            pltpu.VMEM((16, 256, 768), BF),
            pltpu.VMEM((16, 1024, 128), BF),
            pltpu.VMEM((1024, 768), BF),
            pltpu.VMEM((2, 1024, 512), BF),
            pltpu.VMEM((8, 128, 640), F32),
            pltpu.VMEM((3, 4, 2, 64, 1024), F32),
            pltpu.VMEM((3, 4, 2, 64, 1024), BF),
            pltpu.VMEM((2, 4, 64, 1024), BF),
            pltpu.VMEM((4, 2, 2, 64, 1024), BF),
            pltpu.VMEM((32, 16, 1024), BF),
            pltpu.VMEM((32, 16, 1024), BF),
            pltpu.VMEM((16, 128, 256), BF),
            pltpu.VMEM((1024, 768), F32),
            pltpu.SemaphoreType.DMA((4,)),
            pltpu.SemaphoreType.DMA((S_COUNT,)),
            pltpu.SemaphoreType.DMA((M_COUNT,)),
        ],
        compiler_params=pltpu.CompilerParams(
            collective_id=0, has_side_effects=True, vmem_limit_bytes=60 * 1024 * 1024
        ),
    )(tokens, norm_gain.reshape(1, 4096), send_order, segment_ids, w_query, w_key, w_value, w_out)


def solution(mesh):
    return jax.shard_map(
        per_device,
        mesh=mesh,
        in_specs=(
            P(("dp", "seq"), None),
            P(),
            P(("dp", "seq"), None),
            P("dp", None),
            P("dp", "seq"),
            P("dp", None),
            P("dp", None),
            P("seq", "dp"),
        ),
        out_specs=P(("dp", "seq"), None),
        check_vma=False,
    )
```

```python
import jax
import jax.numpy as jnp
from jax import lax
from jax.experimental import pallas as pl
from jax.experimental.pallas import tpu as pltpu
from jax.sharding import PartitionSpec as P

BF = jnp.bfloat16
F32 = jnp.float32
MESH = pl.DeviceIdType.MESH
NEG = float("-inf")
EXP_SCALE = 128 ** (-0.5) * 1.4426950408889634

M_SIB_ROWS = 0
M_SIB_WO = 1
M_SIB_KV = 2
M_SIB_X = 6
M_SIB_HO = 10
M_A2A = 18
M_Z = 34
M_W = 82
M_WO = 114
M_OPP = 146
M_FIN = 147
M_HOME = 151
M_COUNT = 152
S_SIB, S_WO_SIB, S_KV, S_X, S_HO, S_A2A, S_Z, S_W, S_WO, S_OPP, S_FIN, S_HOME, S_COUNT = range(13)

OFFSETS = (
    (0, 0), (1, 0), (3, 0), (0, 1), (0, 3), (2, 0), (0, 2), (1, 1), (3, 3), (1, 3), (3, 1),
    (2, 1), (2, 3), (1, 2), (3, 2), (2, 2),
)


class Gather:
    PLACE = {
        0: (-1, 0), 1: (1, 0), 2: (2, 0), 3: (2, 0), 4: (0, -1), 5: (-1, -1), 6: (1, -1), 7: (2, -1),
        8: (0, 1), 9: (-1, 1), 10: (1, 1), 11: (2, 1), 12: (0, 2), 13: (-1, 2), 14: (1, 2), 15: (2, 2),
    }
    ONWARD = {
        0: ((2, 1, 0), (5, 0, 1), (9, 0, -1)), 1: ((3, -1, 0), (6, 0, 1), (10, 0, -1)),
        3: ((7, 0, 1), (11, 0, -1)), 4: ((12, 0, 1),), 5: ((13, 0, 1),), 10: ((14, 0, -1),), 11: ((15, 0, -1),),
    }

    def __init__(self, base, group, view, rows, at, message):
        self.base, self.group, self.view, self.rows, self.at, self.message = base, group, view, rows, at, message

    def part(self, h, d1, d2, quarter=None):
        half = self.rows // 2
        if quarter is None:
            return self.view(self.at(h, d1, d2), h * half, half)
        return self.view(self.at(h, d1, d2), h * half + quarter * (half // 2), half // 2)

    def send(self, h, m, ref, d1, d2):
        self.message(self.base + 16 * h + m, self.group, ref, ref, (self.at(h, d1, d2), None)).start()

    def own(self, halves=(0, 1)):
        for h in halves:
            mine = self.part(h, 0, 0)
            self.send(h, 0, mine, 1, 0)
            self.send(h, 1, mine, -1, 0)
            self.send(h, 4, mine, 0, 1)
            self.send(h, 8, mine, 0, -1)

    def take(self, *messages, halves=(0, 1)):
        for m in messages:
            for h in halves:
                d1, d2 = self.PLACE[m]
                ref = self.part(h, d1, d2, m - 2 if m in (2, 3) else None)
                self.message(self.base + 16 * h + m, self.group, ref, ref, None).wait_recv()
                for then, s1, s2 in self.ONWARD.get(m, ()):
                    self.send(h, then, self.part(h, d1, d2, then - 2 if then in (2, 3) else None), s1, s2)


def kernel(
    tok, gain, order, seg, wq, wk, wv, wo, out,
    x_buf, nb, sib, s_buf, wall, wob, qkv, ho, bias, p32, snd, opr, fin, fs, r_buf, pick, part,
    lsem, ssem, rsem,
):
    dp = lax.axis_index("dp")
    sq = lax.axis_index("seq")
    x, y = lax.div(dp, 4), lax.rem(dp, 4)
    z, c = lax.div(sq, 2), lax.rem(sq, 2)
    other = 1 - c

    def ring(v):
        return {0: v, 1: lax.rem(v + 1, 4), 2: lax.rem(v + 2, 4), -1: lax.rem(v + 3, 4), 3: lax.rem(v + 3, 4)}

    xr, yr, zr = ring(x), ring(y), ring(z)

    def plane(kx, ky):
        return xr[kx] * 4 + yr[ky]

    def back(kx, ky):
        return xr[(4 - kx) % 4] * 4 + yr[(4 - ky) % 4]

    def half_of(kx, ky):
        return lax.div(lax.rem(ky + 3 * lax.div(kx, 2), 4), 2)

    def message(index, group, src, dst, dev):
        if dev is None:
            dev = (dp, z * 2 + other)
        elif dev[1] is None:
            dev = (dev[0], sq)
        return pltpu.make_async_remote_copy(
            src_ref=src, dst_ref=dst, send_sem=ssem.at[group], recv_sem=rsem.at[index],
            device_id=dev, device_id_type=MESH,
        )

    sibling = (dp, z * 2 + other)
    z_up, z_down = (dp, zr[1] * 2 + c), (dp, zr[-1] * 2 + c)

    barrier = pltpu.get_barrier_semaphore()
    greeted = [sibling, z_up, z_down]
    for kx in range(4):
        for ky in range(4):
            if kx or ky:
                greeted.append((plane(kx, ky), sq))
                greeted.append((plane(kx, ky), z * 2 + other))
    for dev in greeted:
        pl.semaphore_signal(barrier, inc=1, device_id=dev, device_id_type=MESH)

    load_q = pltpu.make_async_copy(wq, wall.at[dp, :, pl.ds(128, 512)], lsem.at[0])
    load_q.start()
    load_o = pltpu.make_async_copy(
        wo.at[:, pl.ds(pl.multiple_of(c * 128, 128), 128)],
        wob.at[dp, pl.ds(pl.multiple_of(c * 512, 512), 512), :], lsem.at[2])
    load_o.start()
    kv_cols = pl.ds(pl.multiple_of(z * 128, 128), 128)
    load_k = pltpu.make_async_copy(wk.at[:, kv_cols], wall.at[dp, :, pl.ds(0, 128)], lsem.at[1])
    load_v = pltpu.make_async_copy(wv.at[:, kv_cols], wall.at[dp, :, pl.ds(640, 128)], lsem.at[1])

    @pl.when(c == 0)
    def _():
        load_k.start()

    @pl.when(c == 1)
    def _():
        load_v.start()

    def norm_rows(i, carry):
        rows = pl.ds(pl.multiple_of(i * 16, 16), 16)
        wide = tok[rows, :].astype(F32)
        square = jnp.mean(wide * wide, axis=1, keepdims=True)
        out[rows, :] = (wide * lax.rsqrt(square + 1e-05) * gain[...]).astype(BF)
        return carry

    lax.fori_loop(0, 8, norm_rows, 0)

    to_home = (order[...] == lax.broadcasted_iota(jnp.int32, (128, 128), 0)).astype(F32)
    to_send = to_home.T.astype(BF)

    def permute(i, carry):
        half, k = lax.div(i, 4), lax.rem(i, 4)
        nb[half, :, pl.ds(pl.multiple_of(k * 512, 512), 512)] = jnp.dot(
            to_send, out[:, pl.ds(pl.multiple_of(i * 512, 512), 512)], preferred_element_type=F32
        ).astype(BF)
        return carry

    lax.fori_loop(0, 8, permute, 0)

    column = lax.broadcasted_iota(jnp.int32, (128, 256), 1)
    source = lax.div(column, 16) * 8 + lax.rem(column, 8)
    spread = lax.broadcasted_iota(jnp.int32, (128, 256), 0) == source
    whence = jnp.dot(to_home.astype(BF), spread.astype(F32).astype(BF), preferred_element_type=F32)
    group_x, group_y = lax.div(column, 64), lax.rem(lax.div(column, 16), 4)
    piece_half = lax.rem(lax.div(column, 8), 2)

    def pick_block(j, carry):
        here = half_of(lax.rem(lax.div(j, 4) - group_x + 4, 4), lax.rem(lax.rem(j, 4) - group_y + 4, 4))
        pick[j] = jnp.where(here == piece_half, whence, 0.0).astype(BF)
        return carry

    lax.fori_loop(0, 16, pick_block, 0)

    def mask_rows(qb, carry):
        seg_q = seg[:, pl.ds(pl.multiple_of(qb * 128, 128), 128)].astype(F32)
        seg_q = jnp.broadcast_to(seg_q, (128, 128)).T
        start = jnp.maximum(qb - 4, 0) * 128
        row_at = qb * 128 + lax.broadcasted_iota(jnp.int32, (128, 128), 0)
        for k in range(5):
            seg_k = seg[:, pl.ds(pl.multiple_of(start + k * 128, 128), 128)].astype(F32)
            col_at = start + k * 128 + lax.broadcasted_iota(jnp.int32, (128, 128), 1)
            visible = (seg_q == seg_k) & (row_at >= col_at)
            bias[qb, :, k * 128 : (k + 1) * 128] = jnp.where(visible, 0.0, NEG)
        return carry

    lax.fori_loop(0, 8, mask_rows, 0)

    @pl.when(c == 0)
    def _():
        load_k.wait()

    @pl.when(c == 1)
    def _():
        load_v.wait()

    load_q.wait()
    pl.semaphore_wait(barrier, len(greeted))

    def at(h, d1, d2):
        return xr[d2] * 4 + yr[d1] if h == 0 else xr[d1] * 4 + yr[d2]

    sib_rows = message(M_SIB_ROWS, S_SIB, nb.at[other], sib, sibling)
    sib_rows.start()
    own_cols = pl.ds(pl.multiple_of(c * 128, 128), 640)
    gather_w = Gather(M_W, S_W, lambda j, lo, n: wall.at[j, pl.ds(lo, n), own_cols], 256, at, message)
    gather_o = Gather(M_WO, S_WO, lambda j, lo, n: wob.at[j, pl.ds(lo, n), :], 1024, at, message)
    gather_w.own(halves=(0,))
    sib_rows.wait_recv()

    def interleave(i, carry):
        cols = pl.ds(pl.multiple_of(i * 256, 256), 256)
        mine = nb[c, :, cols].astype(F32)
        his = sib[:, cols].astype(F32)
        low = jnp.where(c == 0, mine, his).reshape(16, 1, 8, 256)
        high = jnp.where(c == 0, his, mine).reshape(16, 1, 8, 256)
        s_buf[:, cols] = jnp.concatenate([low, high], axis=1).reshape(256, 256).astype(BF)
        return carry

    lax.fori_loop(0, 8, interleave, 0)

    def x_rows(half, zz, row, count):
        return x_buf.at[half, pl.ds(pl.multiple_of(zz * 256 + row, 16), count), :]

    def piece(j):
        return s_buf.at[pl.ds(pl.multiple_of(j * 16, 16), 16), :]

    def scatter(first, last):
        for kx, ky in OFFSETS[first:last]:
            j = plane(kx, ky)
            message(M_A2A + kx * 4 + ky, S_A2A, piece(j), x_rows(c, z, dp * 16, 16), (j, sq)).start()

    scatter(1, 7)
    x_buf[c, pl.ds(pl.multiple_of(z * 256 + dp * 16, 16), 16), :] = s_buf[pl.ds(pl.multiple_of(dp * 16, 16), 16), :]

    def to_sibling(rel, row):
        ref = x_rows(c, zr[rel], row, 16)
        message(M_SIB_X + (rel % 4), S_X, ref, ref, sibling).start()

    def arrived(e):
        kx, ky = OFFSETS[e]
        row = back(kx, ky) * 16
        ref = x_rows(c, z, row, 16)
        if kx or ky:
            message(M_A2A + kx * 4 + ky, S_A2A, ref, ref, None).wait_recv()
        message(M_Z + e, S_Z, ref, ref, z_up).start()
        message(M_Z + 16 + e, S_Z, ref, ref, z_down).start()
        to_sibling(0, row)

    def passed(e):
        row = back(*OFFSETS[e]) * 16
        low = x_rows(c, zr[-1], row, 16)
        message(M_Z + e, S_Z, low, low, None).wait_recv()
        if e % 2 == 0:
            message(M_Z + 32 + e, S_Z, low, low, z_up).start()
        to_sibling(-1, row)
        high = x_rows(c, zr[1], row, 16)
        message(M_Z + 16 + e, S_Z, high, high, None).wait_recv()
        if e % 2 == 1:
            message(M_Z + 32 + e, S_Z, high, high, z_down).start()
        to_sibling(1, row)

    def opposite(e):
        row = back(*OFFSETS[e]) * 16
        ref = x_rows(c, zr[2], row, 16)
        message(M_Z + 32 + e, S_Z, ref, ref, None).wait_recv()
        to_sibling(2, row)

    arrived(0)
    gather_w.own(halves=(1,))
    for e in range(1, 5):
        arrived(e)
    scatter(7, 11)
    wo_slot = wob.at[dp, pl.ds(pl.multiple_of(c * 512, 512), 512), :]
    sib_wo = message(
        M_SIB_WO, S_WO_SIB, wo.at[:, pl.ds(pl.multiple_of(other * 128, 128), 128)], wo_slot, sibling)
    sib_wo.start()
    for e in range(5, 7):
        arrived(e)
    scatter(11, 16)
    gather_w.take(0, 1)
    for e in range(7, 11):
        arrived(e)
    gather_w.take(4, 8)
    for e in range(11, 16):
        arrived(e)

    GROUPS = (
        ((0, 0), (0, 1), (0, -1), (1, 0), (-1, 0)),
        ((0, 2), (2, 0), (1, 1), (1, -1), (-1, 1), (-1, -1)),
        ((2, 1), (2, -1), (1, 2), (-1, 2), (2, 2)),
    )

    def kv_send(q):
        cols = pl.ds(pl.multiple_of(c * 640, 128), 128)
        for kx, ky in GROUPS[q]:
            ref = wall.at[plane(kx, ky), :, cols]
            message(M_SIB_KV + q, S_KV, ref, ref, sibling).start()

    def kv_wait(q):
        ref = wall.at[pl.ds(0, len(GROUPS[q])), :, pl.ds(pl.multiple_of(other * 640, 128), 128)]
        message(M_SIB_KV + q, S_KV, ref, ref, None).wait_recv()

    def sibling_rows(rel):
        ref = x_rows(other, zr[rel], 0, 256)
        message(M_SIB_X + (rel % 4), S_X, ref, ref, None).wait_recv()

    def project(q, first, last):
        blocks = [plane(kx, ky) for kx, ky in GROUPS[q]]

        def columns(i, carry):
            k, n = lax.div(i, 3), lax.rem(i, 3)
            zz = lax.rem(z + k + lax.div(k, 2) - 2 * lax.div(k, 3), 4)
            rows, cols = pl.ds(pl.multiple_of(zz * 256, 256), 256), pl.ds(pl.multiple_of(n * 256, 256), 256)
            acc = part[rows, cols] if q > 0 else 0.0
            for j in blocks:
                features = pl.ds(pl.multiple_of(lax.rem(j, 8) * 256, 256), 256)
                acc += jnp.dot(x_buf[lax.div(j, 8), rows, features], wall[j, :, cols], preferred_element_type=F32)
            if q < 2:
                part[rows, cols] = acc
            else:
                acc = jnp.transpose(acc.reshape(16, 2, 8, 256), (1, 0, 2, 3)).reshape(256, 256)
                qkv[rows, cols] = acc.astype(BF)
            return carry

        lax.fori_loop(3 * first, 3 * last, columns, 0)

    gather_w.take(2, 3, 5, 10)
    kv_send(0)
    for e in range(8):
        passed(e)
    sibling_rows(0)
    kv_wait(0)
    project(0, 0, 1)
    for e in range(8, 16):
        passed(e)
    gather_w.take(12, 6, 9, 11)
    kv_send(1)
    load_o.wait()
    sib_slot = wob.at[dp, pl.ds(pl.multiple_of(other * 512, 512), 512), :]
    message(M_SIB_WO, S_WO_SIB, sib_slot, sib_slot, None).wait_recv()
    gather_o.own()
    sibling_rows(1)
    sibling_rows(-1)
    project(0, 1, 3)
    kv_wait(1)
    project(1, 0, 3)
    for e in range(16):
        opposite(e)
    sibling_rows(2)
    project(0, 3, 4)
    project(1, 3, 4)
    gather_w.take(7, 13, 14, 15)
    kv_send(2)
    gather_o.take(0, 1, 4, 8)
    kv_wait(2)
    project(2, 0, 4)
    gather_o.take(2, 3, 5, 10)

    def attend(i, zz):
        def half_block(half, carry):
            qb = zz * 2 + half
            rows = pl.ds(pl.multiple_of(qb * 128, 128), 128)
            window = pl.ds(pl.multiple_of(jnp.maximum(qb - 4, 0) * 128, 128), 640)
            query = jnp.concatenate([qkv[rows, 128 + 128 * h : 256 + 128 * h] for h in range(4)], axis=0)
            keys, values = qkv[window, 0:128], qkv[window, 640:768]
            scores = lax.dot_general(query, keys, (((1,), (1,)), ((), ())), preferred_element_type=F32)
            scores = scores.reshape(4, 128, 640) + bias[qb][None]
            top = jnp.max(scores, axis=2, keepdims=True)
            weights = jnp.exp2((scores - top) * EXP_SCALE)
            total = jnp.sum(weights, axis=2, keepdims=True).reshape(512, 1)
            mixed = jnp.dot(weights.astype(BF).reshape(512, 640), values, preferred_element_type=F32) / total
            for h in range(4):
                ho[c, rows, 128 * h : 128 * h + 128] = mixed[128 * h : 128 * h + 128].astype(BF)
            message(M_SIB_HO + 2 * i + half, S_HO, ho.at[c, rows, :], ho.at[c, rows, :], sibling).start()
            return carry

        lax.fori_loop(0, 2, half_block, 0)

    def project_out(i, zz, blocks):
        rows = pl.ds(pl.multiple_of(zz * 256, 256), 256)
        lhs = jnp.concatenate([ho[0, rows, :], ho[1, rows, :]], axis=1)
        rhs = [wob[j] for j in blocks]
        acc = jnp.dot(lhs, rhs[0] if len(rhs) == 1 else jnp.concatenate(rhs, axis=1), preferred_element_type=F32)
        acc = jnp.transpose(acc.reshape(2, 16, 8, 128 * len(blocks)), (1, 0, 2, 3)).reshape(16, 16, 128 * len(blocks))
        for n, j in enumerate(blocks):
            bx, by = lax.div(j, 4), lax.rem(j, 4)
            half = half_of(lax.rem(bx - x + 4, 4), lax.rem(by - y + 4, 4))
            cols = pl.ds(pl.multiple_of((bx * 2 + lax.rem(by, 2)) * 128, 128), 128)
            for at_j in range(16):
                kx, ky = lax.rem(at_j // 4 - x + 4, 4), lax.rem(at_j % 4 - y + 4, 4)
                group, at_row = lax.rem(ky - kx + 4, 4), pl.ds(pl.multiple_of(kx * 16, 16), 16)
                val = acc[at_j, :, 128 * n : 128 * n + 128]
                if i > 0:
                    p32[i - 1, group, half, at_row, cols] = val
                if i < 3:
                    snd[i, group, half, at_row, cols] = val.astype(BF)

    def heads_of_sibling(i, zz):
        for half in range(2):
            ref = ho.at[other, pl.ds(pl.multiple_of(zz * 256 + half * 128, 128), 128), :]
            message(M_SIB_HO + 2 * i + half, S_HO, ref, ref, None).wait_recv()

    HALF = lambda kx, ky: ((ky % 4 + 3 * (kx % 4 // 2)) % 4) // 2

    def farthest(q):
        offsets = GROUPS[q]
        for first in range(0, len(offsets), 2):
            project_out(0, zr[2], [plane(kx, ky) for kx, ky in offsets[first : first + 2]])
            for kx, ky in offsets[first : first + 2]:
                half, place = HALF(kx, ky), xr[kx] * 2 + lax.rem(yr[ky], 2)
                cols = pl.ds(pl.multiple_of(place * 128, 128), 128)
                message(
                    M_OPP, S_OPP, snd.at[0, :, half, :, cols], opr.at[half, :, :, cols],
                    z_down if half else z_up).start()

    def fin_message(side, group, half):
        return message(
            M_FIN + group, S_FIN, snd.at[1 + side, group, half], fin.at[group, side, half],
            z_down if side else z_up)

    def project_whole(i, zz):
        heads_of_sibling(i, zz)

        def both(n, carry):
            j = lax.div(n, 2) * 4 + lax.rem(n, 2)
            project_out(i, zz, [j, j + 2])
            return carry

        lax.fori_loop(0, 8, both, 0)

    attend(0, zr[2])
    heads_of_sibling(0, zr[2])
    farthest(0)
    gather_o.take(12, 6, 9)
    farthest(1)
    gather_o.take(11)
    attend(1, zr[1])
    attend(2, zr[-1])
    gather_o.take(7, 13, 14, 15)
    farthest(2)
    project_whole(1, zr[1])
    fin_message(0, 0, 1).start()
    fin_message(0, 1, 1).start()
    project_whole(2, zr[-1])
    fin_message(1, 0, 0).start()
    fin_message(1, 1, 0).start()
    message(M_OPP, S_OPP, opr, opr, None).wait_recv()
    for group in range(4):
        for side in range(2):
            snd[1 + side, group, side] = (p32[side, group, side] + opr[side, group].astype(F32)).astype(BF)
            fin_message(side, group, side).start()
            if group < 2:
                fin_message(side, group + 2, 1 - side).start()
    attend(3, z)
    project_whole(3, z)

    for group in range(4):
        message(M_FIN + group, S_FIN, fin.at[group], fin.at[group], None).wait_recv()

        def total(k, carry):
            rows = pl.ds(pl.multiple_of(k * 16, 16), 16)
            tot = [
                p32[2, group, half, rows, :] + fin[group, 0, half, rows, :].astype(F32)
                + fin[group, 1, half, rows, :].astype(F32)
                for half in range(2)
            ]
            for core in range(2):
                fs[group * 8 + k * 2 + core] = jnp.concatenate(
                    [t[core * 8 : core * 8 + 8] for t in tot], axis=0).astype(BF)
            return carry

        lax.fori_loop(0, 4, total, 0)
        for k in (2, 1, 3, 0):
            for same in range(2):
                core = other if same == 0 else c
                src, dst = fs.at[group * 8 + k * 2 + core], r_buf.at[c * 16 + dp]
                if group or k or same == 0:
                    message(M_HOME, S_HOME, src, dst, (plane(k, (k + group) % 4), z * 2 + core)).start()
                else:
                    keep = pltpu.make_async_copy(src, dst, lsem.at[3])
                    keep.start()

    keep.wait()
    came = r_buf.at[pl.ds(0, 31)]
    message(M_HOME, S_HOME, came, came, None).wait_recv()

    for j in range(16):
        place = (j // 4) * 2 + j % 2
        cols = slice(place * 128, place * 128 + 128)
        rhs = jnp.concatenate([r_buf[16 * core : 16 * core + 16, :, cols].reshape(256, 128) for core in range(2)], axis=1)
        out[:, j * 256 : j * 256 + 256] = jnp.dot(pick[j], rhs, preferred_element_type=F32).astype(BF)

    def sent(group, ref):
        message(0, group, ref, ref, None).wait_send()

    sent(S_SIB, sib)
    sent(S_WO_SIB, wo_slot)
    sent(S_KV, wall.at[:, :, pl.ds(0, 128)])
    sent(S_X, x_buf.at[0])
    sent(S_HO, ho.at[0])
    sent(S_A2A, s_buf.at[pl.ds(0, 240), :])
    sent(S_Z, x_buf.at[0, pl.ds(0, 768), :])
    sent(S_W, wall.at[pl.ds(0, 15), :, pl.ds(0, 640)])
    sent(S_WO, wob.at[pl.ds(0, 15)])
    sent(S_OPP, snd.at[0])
    sent(S_FIN, snd.at[pl.ds(1, 2)])
    sent(S_HOME, fs.at[pl.ds(0, 31)])


def per_device(tokens, norm_gain, send_order, segment_ids, w_query, w_key, w_value, w_out):
    vmem = pl.BlockSpec(memory_space=pltpu.VMEM)
    hbm = pl.BlockSpec(memory_space=pl.ANY)
    return pl.pallas_call(
        kernel,
        out_shape=jax.ShapeDtypeStruct((128, 4096), BF),
        in_specs=[vmem] * 4 + [hbm] * 4,
        out_specs=vmem,
        scratch_shapes=[
            pltpu.VMEM((2, 1024, 2048), BF),
            pltpu.VMEM((2, 128, 2048), BF),
            pltpu.VMEM((128, 2048), BF),
            pltpu.VMEM((256, 2048), BF),
            pltpu.VMEM((16, 256, 768), BF),
            pltpu.VMEM((16, 1024, 128), BF),
            pltpu.VMEM((1024, 768), BF),
            pltpu.VMEM((2, 1024, 512), BF),
            pltpu.VMEM((8, 128, 640), F32),
            pltpu.VMEM((3, 4, 2, 64, 1024), F32),
            pltpu.VMEM((3, 4, 2, 64, 1024), BF),
            pltpu.VMEM((2, 4, 64, 1024), BF),
            pltpu.VMEM((4, 2, 2, 64, 1024), BF),
            pltpu.VMEM((32, 16, 1024), BF),
            pltpu.VMEM((32, 16, 1024), BF),
            pltpu.VMEM((16, 128, 256), BF),
            pltpu.VMEM((1024, 768), F32),
            pltpu.SemaphoreType.DMA((4,)),
            pltpu.SemaphoreType.DMA((S_COUNT,)),
            pltpu.SemaphoreType.DMA((M_COUNT,)),
        ],
        compiler_params=pltpu.CompilerParams(
            collective_id=0, has_side_effects=True, vmem_limit_bytes=60 * 1024 * 1024
        ),
    )(tokens, norm_gain.reshape(1, 4096), send_order, segment_ids, w_query, w_key, w_value, w_out)


def solution(mesh):
    return jax.shard_map(
        per_device,
        mesh=mesh,
        in_specs=(
            P(("dp", "seq"), None),
            P(),
            P(("dp", "seq"), None),
            P("dp", None),
            P("dp", "seq"),
            P("dp", None),
            P("dp", None),
            P("seq", "dp"),
        ),
        out_specs=P(("dp", "seq"), None),
        check_vma=False,
    )
```

```python
import jax
import jax.numpy as jnp
from jax import lax
from jax.experimental import pallas as pl
from jax.experimental.pallas import tpu as pltpu
from jax.sharding import PartitionSpec as P

BF = jnp.bfloat16
F32 = jnp.float32
MESH = pl.DeviceIdType.MESH
NEG = float("-inf")
EXP_SCALE = 128 ** (-0.5) * 1.4426950408889634

M_SIB_ROWS = 0
M_SIB_WO = 1
M_SIB_KV = 2
M_SIB_X = 6
M_SIB_HO = 10
M_A2A = 18
M_Z = 34
M_W = 82
M_WO = 114
M_OPP = 146
M_FIN = 147
M_HOME = 151
M_COUNT = 152
S_SIB, S_WO_SIB, S_KV, S_X, S_HO, S_A2A, S_Z, S_W, S_WO, S_OPP, S_FIN, S_HOME, S_COUNT = range(13)

OFFSETS = (
    (0, 0), (1, 0), (3, 0), (0, 1), (0, 3), (2, 0), (0, 2), (1, 1), (3, 3), (1, 3), (3, 1),
    (2, 1), (2, 3), (1, 2), (3, 2), (2, 2),
)


class Gather:
    PLACE = {
        0: (-1, 0), 1: (1, 0), 2: (2, 0), 3: (2, 0), 4: (0, -1), 5: (-1, -1), 6: (1, -1), 7: (2, -1),
        8: (0, 1), 9: (-1, 1), 10: (1, 1), 11: (2, 1), 12: (0, 2), 13: (-1, 2), 14: (1, 2), 15: (2, 2),
    }
    ONWARD = {
        0: ((2, 1, 0), (5, 0, 1), (9, 0, -1)), 1: ((3, -1, 0), (6, 0, 1), (10, 0, -1)),
        3: ((7, 0, 1), (11, 0, -1)), 4: ((12, 0, 1),), 5: ((13, 0, 1),), 10: ((14, 0, -1),), 11: ((15, 0, -1),),
    }

    def __init__(self, base, group, view, rows, at, message):
        self.base, self.group, self.view, self.rows, self.at, self.message = base, group, view, rows, at, message

    def part(self, h, d1, d2, quarter=None):
        half = self.rows // 2
        if quarter is None:
            return self.view(self.at(h, d1, d2), h * half, half)
        return self.view(self.at(h, d1, d2), h * half + quarter * (half // 2), half // 2)

    def send(self, h, m, ref, d1, d2):
        self.message(self.base + 16 * h + m, self.group, ref, ref, (self.at(h, d1, d2), None)).start()

    def own(self, halves=(0, 1)):
        for h in halves:
            mine = self.part(h, 0, 0)
            self.send(h, 0, mine, 1, 0)
            self.send(h, 1, mine, -1, 0)
            self.send(h, 4, mine, 0, 1)
            self.send(h, 8, mine, 0, -1)

    def take(self, *messages, halves=(0, 1)):
        for m in messages:
            for h in halves:
                d1, d2 = self.PLACE[m]
                ref = self.part(h, d1, d2, m - 2 if m in (2, 3) else None)
                self.message(self.base + 16 * h + m, self.group, ref, ref, None).wait_recv()
                for then, s1, s2 in self.ONWARD.get(m, ()):
                    self.send(h, then, self.part(h, d1, d2, then - 2 if then in (2, 3) else None), s1, s2)


def kernel(
    tok, gain, order, seg, wq, wk, wv, wo, out,
    x_buf, nb, sib, s_buf, wall, wob, qkv, ho, bias, p32, snd, opr, fin, fs, r_buf, pick, part,
    lsem, ssem, rsem,
):
    dp = lax.axis_index("dp")
    sq = lax.axis_index("seq")
    x, y = lax.div(dp, 4), lax.rem(dp, 4)
    z, c = lax.div(sq, 2), lax.rem(sq, 2)
    other = 1 - c

    def ring(v):
        return {0: v, 1: lax.rem(v + 1, 4), 2: lax.rem(v + 2, 4), -1: lax.rem(v + 3, 4), 3: lax.rem(v + 3, 4)}

    xr, yr, zr = ring(x), ring(y), ring(z)

    def plane(kx, ky):
        return xr[kx] * 4 + yr[ky]

    def back(kx, ky):
        return xr[(4 - kx) % 4] * 4 + yr[(4 - ky) % 4]

    def half_of(kx, ky):
        return lax.div(lax.rem(ky + 3 * lax.div(kx, 2), 4), 2)

    def message(index, group, src, dst, dev):
        if dev is None:
            dev = (dp, z * 2 + other)
        elif dev[1] is None:
            dev = (dev[0], sq)
        return pltpu.make_async_remote_copy(
            src_ref=src, dst_ref=dst, send_sem=ssem.at[group], recv_sem=rsem.at[index],
            device_id=dev, device_id_type=MESH,
        )

    sibling = (dp, z * 2 + other)
    z_up, z_down = (dp, zr[1] * 2 + c), (dp, zr[-1] * 2 + c)

    barrier = pltpu.get_barrier_semaphore()
    greeted = [sibling, z_up, z_down]
    for kx in range(4):
        for ky in range(4):
            if kx or ky:
                greeted.append((plane(kx, ky), sq))
                greeted.append((plane(kx, ky), z * 2 + other))
    for dev in greeted:
        pl.semaphore_signal(barrier, inc=1, device_id=dev, device_id_type=MESH)

    load_q = pltpu.make_async_copy(wq, wall.at[dp, :, pl.ds(128, 512)], lsem.at[0])
    load_q.start()
    load_o = pltpu.make_async_copy(
        wo.at[:, pl.ds(pl.multiple_of(c * 128, 128), 128)],
        wob.at[dp, pl.ds(pl.multiple_of(c * 512, 512), 512), :], lsem.at[2])
    load_o.start()
    kv_cols = pl.ds(pl.multiple_of(z * 128, 128), 128)
    load_k = pltpu.make_async_copy(wk.at[:, kv_cols], wall.at[dp, :, pl.ds(0, 128)], lsem.at[1])
    load_v = pltpu.make_async_copy(wv.at[:, kv_cols], wall.at[dp, :, pl.ds(640, 128)], lsem.at[1])

    @pl.when(c == 0)
    def _():
        load_k.start()

    @pl.when(c == 1)
    def _():
        load_v.start()

    def norm_rows(i, carry):
        rows = pl.ds(pl.multiple_of(i * 16, 16), 16)
        wide = tok[rows, :].astype(F32)
        square = jnp.mean(wide * wide, axis=1, keepdims=True)
        out[rows, :] = (wide * lax.rsqrt(square + 1e-05) * gain[...]).astype(BF)
        return carry

    lax.fori_loop(0, 8, norm_rows, 0)

    to_home = (order[...] == lax.broadcasted_iota(jnp.int32, (128, 128), 0)).astype(F32)
    to_send = to_home.T.astype(BF)

    def permute(i, carry):
        half, k = lax.div(i, 4), lax.rem(i, 4)
        nb[half, :, pl.ds(pl.multiple_of(k * 512, 512), 512)] = jnp.dot(
            to_send, out[:, pl.ds(pl.multiple_of(i * 512, 512), 512)], preferred_element_type=F32
        ).astype(BF)
        return carry

    lax.fori_loop(0, 8, permute, 0)

    column = lax.broadcasted_iota(jnp.int32, (128, 256), 1)
    source = lax.div(column, 16) * 8 + lax.rem(column, 8)
    spread = lax.broadcasted_iota(jnp.int32, (128, 256), 0) == source
    whence = jnp.dot(to_home.astype(BF), spread.astype(F32).astype(BF), preferred_element_type=F32)
    group_x, group_y = lax.div(column, 64), lax.rem(lax.div(column, 16), 4)
    piece_half = lax.rem(lax.div(column, 8), 2)

    def pick_block(j, carry):
        here = half_of(lax.rem(lax.div(j, 4) - group_x + 4, 4), lax.rem(lax.rem(j, 4) - group_y + 4, 4))
        pick[j] = jnp.where(here == piece_half, whence, 0.0).astype(BF)
        return carry

    lax.fori_loop(0, 16, pick_block, 0)

    def mask_rows(qb, carry):
        seg_q = seg[:, pl.ds(pl.multiple_of(qb * 128, 128), 128)].astype(F32)
        seg_q = jnp.broadcast_to(seg_q, (128, 128)).T
        start = jnp.maximum(qb - 4, 0) * 128
        row_at = qb * 128 + lax.broadcasted_iota(jnp.int32, (128, 128), 0)
        for k in range(5):
            seg_k = seg[:, pl.ds(pl.multiple_of(start + k * 128, 128), 128)].astype(F32)
            col_at = start + k * 128 + lax.broadcasted_iota(jnp.int32, (128, 128), 1)
            visible = (seg_q == seg_k) & (row_at >= col_at)
            bias[qb, :, k * 128 : (k + 1) * 128] = jnp.where(visible, 0.0, NEG)
        return carry

    lax.fori_loop(0, 8, mask_rows, 0)

    @pl.when(c == 0)
    def _():
        load_k.wait()

    @pl.when(c == 1)
    def _():
        load_v.wait()

    load_q.wait()
    pl.semaphore_wait(barrier, len(greeted))

    def at(h, d1, d2):
        return xr[d2] * 4 + yr[d1] if h == 0 else xr[d1] * 4 + yr[d2]

    sib_rows = message(M_SIB_ROWS, S_SIB, nb.at[other], sib, sibling)
    sib_rows.start()
    own_cols = pl.ds(pl.multiple_of(c * 128, 128), 640)
    gather_w = Gather(M_W, S_W, lambda j, lo, n: wall.at[j, pl.ds(lo, n), own_cols], 256, at, message)
    gather_o = Gather(M_WO, S_WO, lambda j, lo, n: wob.at[j, pl.ds(lo, n), :], 1024, at, message)
    gather_w.own(halves=(0,))
    sib_rows.wait_recv()

    def interleave(i, carry):
        cols = pl.ds(pl.multiple_of(i * 256, 256), 256)
        mine = nb[c, :, cols].astype(F32)
        his = sib[:, cols].astype(F32)
        low = jnp.where(c == 0, mine, his).reshape(16, 1, 8, 256)
        high = jnp.where(c == 0, his, mine).reshape(16, 1, 8, 256)
        s_buf[:, cols] = jnp.concatenate([low, high], axis=1).reshape(256, 256).astype(BF)
        return carry

    lax.fori_loop(0, 8, interleave, 0)

    def x_rows(half, zz, row, count):
        return x_buf.at[half, pl.ds(pl.multiple_of(zz * 256 + row, 16), count), :]

    def piece(j):
        return s_buf.at[pl.ds(pl.multiple_of(j * 16, 16), 16), :]

    def scatter(first, last):
        for kx, ky in OFFSETS[first:last]:
            j = plane(kx, ky)
            message(M_A2A + kx * 4 + ky, S_A2A, piece(j), x_rows(c, z, dp * 16, 16), (j, sq)).start()

    scatter(1, 7)
    x_buf[c, pl.ds(pl.multiple_of(z * 256 + dp * 16, 16), 16), :] = s_buf[pl.ds(pl.multiple_of(dp * 16, 16), 16), :]

    def to_sibling(rel, row):
        ref = x_rows(c, zr[rel], row, 16)
        message(M_SIB_X + (rel % 4), S_X, ref, ref, sibling).start()

    def arrived(e):
        kx, ky = OFFSETS[e]
        row = back(kx, ky) * 16
        ref = x_rows(c, z, row, 16)
        if kx or ky:
            message(M_A2A + kx * 4 + ky, S_A2A, ref, ref, None).wait_recv()
        message(M_Z + e, S_Z, ref, ref, z_up).start()
        message(M_Z + 16 + e, S_Z, ref, ref, z_down).start()
        to_sibling(0, row)

    def passed(e):
        row = back(*OFFSETS[e]) * 16
        low = x_rows(c, zr[-1], row, 16)
        message(M_Z + e, S_Z, low, low, None).wait_recv()
        if e % 2 == 0:
            message(M_Z + 32 + e, S_Z, low, low, z_up).start()
        to_sibling(-1, row)
        high = x_rows(c, zr[1], row, 16)
        message(M_Z + 16 + e, S_Z, high, high, None).wait_recv()
        if e % 2 == 1:
            message(M_Z + 32 + e, S_Z, high, high, z_down).start()
        to_sibling(1, row)

    def opposite(e):
        row = back(*OFFSETS[e]) * 16
        ref = x_rows(c, zr[2], row, 16)
        message(M_Z + 32 + e, S_Z, ref, ref, None).wait_recv()
        to_sibling(2, row)

    arrived(0)
    gather_w.own(halves=(1,))
    for e in range(1, 5):
        arrived(e)
    scatter(7, 11)
    wo_slot = wob.at[dp, pl.ds(pl.multiple_of(c * 512, 512), 512), :]
    sib_wo = message(
        M_SIB_WO, S_WO_SIB, wo.at[:, pl.ds(pl.multiple_of(other * 128, 128), 128)], wo_slot, sibling)
    sib_wo.start()
    for e in range(5, 7):
        arrived(e)
    scatter(11, 16)
    gather_w.take(0, 1)
    for e in range(7, 11):
        arrived(e)
    gather_w.take(4, 8)
    for e in range(11, 16):
        arrived(e)

    GROUPS = (
        ((0, 0), (0, 1), (0, -1), (1, 0), (-1, 0)),
        ((0, 2), (2, 0), (1, 1), (1, -1), (-1, 1), (-1, -1)),
        ((2, 1), (2, -1), (1, 2), (-1, 2), (2, 2)),
    )

    def kv_send(q):
        cols = pl.ds(pl.multiple_of(c * 640, 128), 128)
        for kx, ky in GROUPS[q]:
            ref = wall.at[plane(kx, ky), :, cols]
            message(M_SIB_KV + q, S_KV, ref, ref, sibling).start()

    def kv_wait(q):
        ref = wall.at[pl.ds(0, len(GROUPS[q])), :, pl.ds(pl.multiple_of(other * 640, 128), 128)]
        message(M_SIB_KV + q, S_KV, ref, ref, None).wait_recv()

    def sibling_rows(rel):
        ref = x_rows(other, zr[rel], 0, 256)
        message(M_SIB_X + (rel % 4), S_X, ref, ref, None).wait_recv()

    def project(q, first, last):
        blocks = [plane(kx, ky) for kx, ky in GROUPS[q]]

        def columns(i, carry):
            k, n = lax.div(i, 3), lax.rem(i, 3)
            zz = lax.rem(z + k + lax.div(k, 2) - 2 * lax.div(k, 3), 4)
            rows, cols = pl.ds(pl.multiple_of(zz * 256, 256), 256), pl.ds(pl.multiple_of(n * 256, 256), 256)
            acc = part[rows, cols] if q > 0 else 0.0
            for j in blocks:
                features = pl.ds(pl.multiple_of(lax.rem(j, 8) * 256, 256), 256)
                acc += jnp.dot(x_buf[lax.div(j, 8), rows, features], wall[j, :, cols], preferred_element_type=F32)
            if q < 2:
                part[rows, cols] = acc
            else:
                acc = jnp.transpose(acc.reshape(16, 2, 8, 256), (1, 0, 2, 3)).reshape(256, 256)
                qkv[rows, cols] = acc.astype(BF)
            return carry

        lax.fori_loop(3 * first, 3 * last, columns, 0)

    gather_w.take(2, 3, 5, 10)
    kv_send(0)
    for e in range(8):
        passed(e)
    sibling_rows(0)
    kv_wait(0)
    project(0, 0, 1)
    for e in range(8, 16):
        passed(e)
    gather_w.take(12, 6, 9, 11)
    kv_send(1)
    load_o.wait()
    sib_slot = wob.at[dp, pl.ds(pl.multiple_of(other * 512, 512), 512), :]
    message(M_SIB_WO, S_WO_SIB, sib_slot, sib_slot, None).wait_recv()
    gather_o.own()
    sibling_rows(1)
    sibling_rows(-1)
    project(0, 1, 3)
    kv_wait(1)
    project(1, 0, 3)
    for e in range(16):
        opposite(e)
    sibling_rows(2)
    project(0, 3, 4)
    project(1, 3, 4)
    gather_w.take(7, 13, 14, 15)
    kv_send(2)
    gather_o.take(0, 1, 4, 8)
    kv_wait(2)
    project(2, 0, 4)
    gather_o.take(2, 3, 5, 10)

    def attend(i, zz):
        def half_block(half, carry):
            qb = zz * 2 + half
            rows = pl.ds(pl.multiple_of(qb * 128, 128), 128)
            window = pl.ds(pl.multiple_of(jnp.maximum(qb - 4, 0) * 128, 128), 640)
            query = jnp.concatenate([qkv[rows, 128 + 128 * h : 256 + 128 * h] for h in range(4)], axis=0)
            keys, values = qkv[window, 0:128], qkv[window, 640:768]
            scores = lax.dot_general(query, keys, (((1,), (1,)), ((), ())), preferred_element_type=F32)
            scores = scores.reshape(4, 128, 640) + bias[qb][None]
            top = jnp.max(scores, axis=2, keepdims=True)
            weights = jnp.exp2((scores - top) * EXP_SCALE)
            total = jnp.sum(weights, axis=2, keepdims=True).reshape(512, 1)
            mixed = jnp.dot(weights.astype(BF).reshape(512, 640), values, preferred_element_type=F32) / total
            for h in range(4):
                ho[c, rows, 128 * h : 128 * h + 128] = mixed[128 * h : 128 * h + 128].astype(BF)
            message(M_SIB_HO + 2 * i + half, S_HO, ho.at[c, rows, :], ho.at[c, rows, :], sibling).start()
            return carry

        lax.fori_loop(0, 2, half_block, 0)

    def project_out(i, zz, blocks):
        rows = pl.ds(pl.multiple_of(zz * 256, 256), 256)
        lhs = jnp.concatenate([ho[0, rows, :], ho[1, rows, :]], axis=1)
        rhs = [wob[j] for j in blocks]
        acc = jnp.dot(lhs, rhs[0] if len(rhs) == 1 else jnp.concatenate(rhs, axis=1), preferred_element_type=F32)
        acc = jnp.transpose(acc.reshape(2, 16, 8, 128 * len(blocks)), (1, 0, 2, 3)).reshape(16, 16, 128 * len(blocks))
        for n, j in enumerate(blocks):
            bx, by = lax.div(j, 4), lax.rem(j, 4)
            half = half_of(lax.rem(bx - x + 4, 4), lax.rem(by - y + 4, 4))
            cols = pl.ds(pl.multiple_of((bx * 2 + lax.rem(by, 2)) * 128, 128), 128)
            for at_j in range(16):
                kx, ky = lax.rem(at_j // 4 - x + 4, 4), lax.rem(at_j % 4 - y + 4, 4)
                group, at_row = lax.rem(ky - kx + 4, 4), pl.ds(pl.multiple_of(kx * 16, 16), 16)
                val = acc[at_j, :, 128 * n : 128 * n + 128]
                if i > 0:
                    p32[i - 1, group, half, at_row, cols] = val
                if i < 3:
                    snd[i, group, half, at_row, cols] = val.astype(BF)

    def heads_of_sibling(i, zz):
        for half in range(2):
            ref = ho.at[other, pl.ds(pl.multiple_of(zz * 256 + half * 128, 128), 128), :]
            message(M_SIB_HO + 2 * i + half, S_HO, ref, ref, None).wait_recv()

    HALF = lambda kx, ky: ((ky % 4 + 3 * (kx % 4 // 2)) % 4) // 2

    def farthest(q):
        offsets = GROUPS[q]
        for first in range(0, len(offsets), 2):
            project_out(0, zr[2], [plane(kx, ky) for kx, ky in offsets[first : first + 2]])
            for kx, ky in offsets[first : first + 2]:
                half, place = HALF(kx, ky), xr[kx] * 2 + lax.rem(yr[ky], 2)
                cols = pl.ds(pl.multiple_of(place * 128, 128), 128)
                message(
                    M_OPP, S_OPP, snd.at[0, :, half, :, cols], opr.at[half, :, :, cols],
                    z_down if half else z_up).start()

    def fin_message(side, group, half):
        return message(
            M_FIN + group, S_FIN, snd.at[1 + side, group, half], fin.at[group, side, half],
            z_down if side else z_up)

    def project_half(i, zz, half):
        def one(bx, carry):
            blocks = []
            for by in range(2):
                first = half_of(lax.rem(bx - x + 4, 4), lax.rem(by - y + 4, 4))
                blocks.append(bx * 4 + by + 2 * lax.rem(first + half, 2))
            project_out(i, zz, blocks)
            return carry

        lax.fori_loop(0, 4, one, 0)

    def project_whole(i, zz):
        heads_of_sibling(i, zz)

        def both(n, carry):
            j = lax.div(n, 2) * 4 + lax.rem(n, 2)
            project_out(i, zz, [j, j + 2])
            return carry

        lax.fori_loop(0, 8, both, 0)

    attend(0, zr[2])
    heads_of_sibling(0, zr[2])
    farthest(0)
    gather_o.take(12, 6, 9)
    farthest(1)
    gather_o.take(11)
    attend(1, zr[1])
    attend(2, zr[-1])
    gather_o.take(7, 13, 14, 15)
    farthest(2)
    heads_of_sibling(1, zr[1])
    project_half(1, zr[1], 1)
    fin_message(0, 0, 1).start()
    fin_message(0, 1, 1).start()
    heads_of_sibling(2, zr[-1])
    project_half(2, zr[-1], 0)
    fin_message(1, 0, 0).start()
    fin_message(1, 1, 0).start()
    project_half(1, zr[1], 0)
    project_half(2, zr[-1], 1)
    message(M_OPP, S_OPP, opr, opr, None).wait_recv()
    for group in range(4):
        for side in range(2):
            snd[1 + side, group, side] = (p32[side, group, side] + opr[side, group].astype(F32)).astype(BF)
            fin_message(side, group, side).start()
            if group < 2:
                fin_message(side, group + 2, 1 - side).start()
    attend(3, z)
    project_whole(3, z)

    for group in range(4):
        message(M_FIN + group, S_FIN, fin.at[group], fin.at[group], None).wait_recv()

        def total(k, carry):
            rows = pl.ds(pl.multiple_of(k * 16, 16), 16)
            tot = [
                p32[2, group, half, rows, :] + fin[group, 0, half, rows, :].astype(F32)
                + fin[group, 1, half, rows, :].astype(F32)
                for half in range(2)
            ]
            for core in range(2):
                fs[group * 8 + k * 2 + core] = jnp.concatenate(
                    [t[core * 8 : core * 8 + 8] for t in tot], axis=0).astype(BF)
            return carry

        lax.fori_loop(0, 4, total, 0)
        for k in (2, 1, 3, 0):
            for same in range(2):
                core = other if same == 0 else c
                src, dst = fs.at[group * 8 + k * 2 + core], r_buf.at[c * 16 + dp]
                if group or k or same == 0:
                    message(M_HOME, S_HOME, src, dst, (plane(k, (k + group) % 4), z * 2 + core)).start()
                else:
                    keep = pltpu.make_async_copy(src, dst, lsem.at[3])
                    keep.start()

    keep.wait()
    came = r_buf.at[pl.ds(0, 31)]
    message(M_HOME, S_HOME, came, came, None).wait_recv()

    for j in range(16):
        place = (j // 4) * 2 + j % 2
        cols = slice(place * 128, place * 128 + 128)
        rhs = jnp.concatenate([r_buf[16 * core : 16 * core + 16, :, cols].reshape(256, 128) for core in range(2)], axis=1)
        out[:, j * 256 : j * 256 + 256] = jnp.dot(pick[j], rhs, preferred_element_type=F32).astype(BF)

    def sent(group, ref):
        message(0, group, ref, ref, None).wait_send()

    sent(S_SIB, sib)
    sent(S_WO_SIB, wo_slot)
    sent(S_KV, wall.at[:, :, pl.ds(0, 128)])
    sent(S_X, x_buf.at[0])
    sent(S_HO, ho.at[0])
    sent(S_A2A, s_buf.at[pl.ds(0, 240), :])
    sent(S_Z, x_buf.at[0, pl.ds(0, 768), :])
    sent(S_W, wall.at[pl.ds(0, 15), :, pl.ds(0, 640)])
    sent(S_WO, wob.at[pl.ds(0, 15)])
    sent(S_OPP, snd.at[0])
    sent(S_FIN, snd.at[pl.ds(1, 2)])
    sent(S_HOME, fs.at[pl.ds(0, 31)])


def per_device(tokens, norm_gain, send_order, segment_ids, w_query, w_key, w_value, w_out):
    vmem = pl.BlockSpec(memory_space=pltpu.VMEM)
    hbm = pl.BlockSpec(memory_space=pl.ANY)
    return pl.pallas_call(
        kernel,
        out_shape=jax.ShapeDtypeStruct((128, 4096), BF),
        in_specs=[vmem] * 4 + [hbm] * 4,
        out_specs=vmem,
        scratch_shapes=[
            pltpu.VMEM((2, 1024, 2048), BF),
            pltpu.VMEM((2, 128, 2048), BF),
            pltpu.VMEM((128, 2048), BF),
            pltpu.VMEM((256, 2048), BF),
            pltpu.VMEM((16, 256, 768), BF),
            pltpu.VMEM((16, 1024, 128), BF),
            pltpu.VMEM((1024, 768), BF),
            pltpu.VMEM((2, 1024, 512), BF),
            pltpu.VMEM((8, 128, 640), F32),
            pltpu.VMEM((3, 4, 2, 64, 1024), F32),
            pltpu.VMEM((3, 4, 2, 64, 1024), BF),
            pltpu.VMEM((2, 4, 64, 1024), BF),
            pltpu.VMEM((4, 2, 2, 64, 1024), BF),
            pltpu.VMEM((32, 16, 1024), BF),
            pltpu.VMEM((32, 16, 1024), BF),
            pltpu.VMEM((16, 128, 256), BF),
            pltpu.VMEM((1024, 768), F32),
            pltpu.SemaphoreType.DMA((4,)),
            pltpu.SemaphoreType.DMA((S_COUNT,)),
            pltpu.SemaphoreType.DMA((M_COUNT,)),
        ],
        compiler_params=pltpu.CompilerParams(
            collective_id=0, has_side_effects=True, vmem_limit_bytes=60 * 1024 * 1024
        ),
    )(tokens, norm_gain.reshape(1, 4096), send_order, segment_ids, w_query, w_key, w_value, w_out)


def solution(mesh):
    return jax.shard_map(
        per_device,
        mesh=mesh,
        in_specs=(
            P(("dp", "seq"), None),
            P(),
            P(("dp", "seq"), None),
            P("dp", None),
            P("dp", "seq"),
            P("dp", None),
            P("dp", None),
            P("seq", "dp"),
        ),
        out_specs=P(("dp", "seq"), None),
        check_vma=False,
    )
```
